1024 devices in a mesh: dp: 64 (over x_lo, y, core), fsdp: 16 (over x_hi, z).
Axes of the slice: x: 8 (x_hi: 2, x_lo: 4; x = x_hi * 4 + x_lo), y: 8, z: 8, core: 2. Of those that a mesh axis runs over, the one named last changes fastest.
Arguments:
- pooled_feats: bfloat16 [8192, 1536], P('dp', 'fsdp'), may hold values from -6 to 6
- head_weight: bfloat16 [1536, 1536], P('fsdp'), may hold values from -0.15625 to 0.15625
- text_embed: bfloat16 [8192, 1536], P(('dp', 'fsdp')), may hold values from -6 to 6
- logit_scale: float32 [1], replicated, may hold values from 8 to 16
- logit_bias: float32 [1], replicated, may hold values from -4 to -1
Outputs:
- loss_rows: float32 [8192], P('dp')
- head_grad: float32 [1536, 1536], P('fsdp', 'dp')
- pooled_grad: float32 [8192, 1536], P('dp', 'fsdp')
- text_grad: float32 [8192, 1536], P(('dp', 'fsdp'))
The draws below stay inside these ranges and needn't reach their ends.
All inputs are finite; a program needn't handle non-finite values.
Results may differ from the reference program's by a relative error of at most 0.0052.
Values may be sent and summed in bfloat16 or wider, within the bound.
No kernel may reach another device: no remote copies, remote signals or barrier semaphores. Data moves between devices by JAX's collectives and lax.ppermute only.
A program may use at most 32 MiB of HBM per device.

```python
import math
import jax
import jax.numpy as jnp
from jax import lax

D = 1536
EMB = 1536
GROUP = 128
BATCH = 8192


def block_scale(own_key, dims, pieces, smallest, top_value):
    factor_of = 1.0
    for dim, shards_of in pieces:
        draws = jax.random.uniform(jax.random.fold_in(jax.random.fold_in(own_key, 6), dim), (shards_of,), jnp.float32, smallest / len(pieces), top_value / len(pieces))
        factor_of = factor_of * jnp.repeat(jnp.exp(draws), dims[dim] // shards_of).reshape((-1,) + (1,) * (len(dims) - 1 - dim))
    return factor_of


def gaussian(key, shape, deviation, most, split=(), kind=jnp.bfloat16):
    gain = block_scale(key, shape, split, -0.22, 0.18) if split else 1.0
    values = jax.random.normal(key, shape, jnp.float32) * deviation * gain
    return jnp.minimum(jnp.maximum(values, -most), most).astype(kind)


def setup_inputs(seed: int = 0) -> dict:
    seeds = jax.random.split(jax.random.key(seed), 6)
    pooled_feats = gaussian(seeds[0], (BATCH, D), 1.0, 6.0, ((0, 64), (1, 16)))
    head_weight = gaussian(seeds[1], (D, EMB), D ** -0.5, 0.15625, ((0, 16),))
    text_embed = gaussian(seeds[2], (BATCH, EMB), 1.0, 6.0, ((0, 1024),))
    logit_scale = jnp.clip(jnp.exp(jax.random.uniform(seeds[3], (1,), jnp.float32, math.log(8.0), math.log(16.0))), 8.0, 16.0)
    logit_bias = jnp.clip(jax.random.uniform(seeds[4], (1,), jnp.float32, -4.0, -1.0), -4.0, -1.0)
    return dict(pooled_feats=pooled_feats, head_weight=head_weight, text_embed=text_embed, logit_scale=logit_scale, logit_bias=logit_bias)


epsilon = 1e-06

def reference(pooled_feats, head_weight, text_embed, logit_scale, logit_bias):
    temper = logit_scale[0]
    offset = logit_bias[0]
    image_raw = jnp.dot(pooled_feats, head_weight, preferred_element_type=jnp.float32)
    lengths = jnp.sqrt(lax.optimization_barrier(jnp.sum(image_raw * image_raw, axis=1)) + epsilon)
    image_hat = image_raw / lengths[:, None]
    image_unit = image_hat.astype(jnp.bfloat16)
    text_float = text_embed.astype(jnp.float32)
    text_unit = (text_float / jnp.sqrt(lax.optimization_barrier(jnp.sum(text_float * text_float, axis=1)) + epsilon)[:, None]).astype(jnp.bfloat16)
    block_count = BATCH // GROUP
    image_blocks = image_unit.reshape(block_count, GROUP, EMB)
    col_ids = jnp.arange(BATCH, dtype=jnp.int32)

    def block_step(text_acc, inputs):
        block_id, rows_unit = inputs
        scores = jnp.dot(rows_unit, text_unit.T, preferred_element_type=jnp.float32)
        logits = temper * scores + offset
        row_ids = block_id * GROUP + jnp.arange(GROUP, dtype=jnp.int32)
        labels = jnp.where(row_ids[:, None] == col_ids[None, :], 1.0, -1.0).astype(jnp.float32)
        losses = lax.optimization_barrier(jnp.sum(jax.nn.softplus(-labels * logits), axis=1))
        weights = (-labels * jax.nn.sigmoid(-labels * logits) * temper).astype(jnp.bfloat16)
        image_dir = jnp.dot(weights, text_unit, preferred_element_type=jnp.float32)
        text_acc = text_acc + jnp.dot(weights.T, rows_unit, preferred_element_type=jnp.float32)
        return (text_acc, (losses, image_dir))
    text_grad, outputs = lax.scan(block_step, jnp.zeros((BATCH, EMB), jnp.float32), (jnp.arange(block_count, dtype=jnp.int32), image_blocks))
    loss_rows = outputs[0].reshape(BATCH)
    image_dir = outputs[1].reshape(BATCH, EMB)
    projected = lax.optimization_barrier(jnp.sum(image_hat * image_dir, axis=1))
    unit_grad = ((image_dir - image_hat * projected[:, None]) / lengths[:, None]).astype(jnp.bfloat16)
    head_grad = jnp.dot(pooled_feats.T, unit_grad, preferred_element_type=jnp.float32)
    pooled_grad = jnp.dot(unit_grad, head_weight.T, preferred_element_type=jnp.float32)
    return (loss_rows, head_grad, pooled_grad, text_grad)
```

```python
import functools

import jax
import jax.numpy as jnp
from jax import lax
from jax.experimental import pallas as pl
from jax.experimental.pallas import tpu as pltpu
from jax.sharding import PartitionSpec as P

epsilon = 1e-06
bf16 = jnp.bfloat16
f32 = jnp.float32
VM = pl.BlockSpec(memory_space=pltpu.VMEM)
SM = pl.BlockSpec(memory_space=pltpu.SMEM)
PARAMS = pltpu.CompilerParams(vmem_limit_bytes=40 * 1024 * 1024)


def call(kernel, outs, in_specs, args):
    return pl.pallas_call(
        kernel,
        out_shape=[jax.ShapeDtypeStruct(s, d) for s, d in outs],
        in_specs=in_specs,
        out_specs=[VM] * len(outs),
        compiler_params=PARAMS,
    )(*args)


def swapped(value):
    count = lax.axis_size("dp")
    return lax.ppermute(value, "dp", [(s, s ^ 1) for s in range(count)])


def same_core(value):
    count = lax.axis_size("dp")
    groups = [list(range(c, count, 2)) for c in range(2)]
    return lax.all_to_all(value, "dp", 0, 0, axis_index_groups=groups, tiled=True)


def over_fsdp(value):
    return lax.all_to_all(value, "fsdp", 0, 0, tiled=True)


def front_kernel(feats, weight, text, part, spread):
    part[...] = jnp.dot(feats[...], weight[...], preferred_element_type=f32).astype(part.dtype)
    t = text[...].astype(f32)
    t = t / jnp.sqrt(jnp.sum(t * t, axis=1, keepdims=True) + epsilon)
    spread[...] = jnp.broadcast_to(t.astype(bf16)[None], spread.shape)


def unit_kernel(parts, hat, lengths, spread):
    raw = jnp.sum(parts[...].astype(f32), axis=0)
    size = jnp.sqrt(jnp.sum(raw * raw, axis=1, keepdims=True) + epsilon)
    value = raw / size
    hat[...] = value
    lengths[...] = jnp.broadcast_to(size, lengths.shape)
    spread[...] = jnp.broadcast_to(value.astype(bf16)[None], spread.shape)


def pair_kernel(scalars, where, units, own, other, image, text_own, text_other):
    width = units.shape[1]
    temper, offset = scalars[0], scalars[1]
    chip, member, each = where[0], where[1], where[2]
    rows = units[...]
    total = None
    losses = None
    for half, (texts, out) in enumerate(((own, text_own), (other, text_other))):
        block = texts[...]
        scores = lax.dot_general(
            rows, block, (((1,), (1,)), ((), ())), preferred_element_type=f32
        )
        logits = temper * scores + offset
        if half == 0:
            row = lax.broadcasted_iota(jnp.int32, logits.shape, 0) - member * each
            col = lax.broadcasted_iota(jnp.int32, logits.shape, 1) - chip * each
            positive = (row == col) & (col >= 0) & (col < each)
            sign = jnp.where(positive, -1.0, 1.0).astype(f32)
            logits = sign * logits
        small = jnp.exp(-jnp.abs(logits))
        loss = jnp.sum(jnp.maximum(logits, 0.0) + jnp.log1p(small), axis=1, keepdims=True)
        weights = jnp.where(logits >= 0, 1.0, small) / (1.0 + small) * temper
        if half == 0:
            weights = weights * sign
        weights = weights.astype(bf16)
        part = jnp.dot(weights, block, preferred_element_type=f32)
        out[...] = lax.dot_general(
            weights, rows, (((0,), (0,)), ((), ())), preferred_element_type=f32
        ).astype(out.dtype)
        total = part if half == 0 else total + part
        losses = loss if half == 0 else losses + loss
    image[:, :width] = total.astype(bf16)
    high = losses.astype(bf16).astype(f32)
    low = losses - high
    lane = lax.broadcasted_iota(jnp.int32, (rows.shape[0], 128), 1)
    image[:, width:] = jnp.where(lane == 0, high, jnp.where(lane == 1, low, 0.0)).astype(bf16)


def grad_kernel(parts, hat, lengths, spread):
    width = hat.shape[1]
    total = jnp.sum(parts[...].astype(f32), axis=0)
    direction = total[:, :width]
    value = hat[...]
    projected = jnp.sum(value * direction, axis=1, keepdims=True)
    grad = (direction - value * projected) / lengths[:, :1]
    spread[:, :, :width] = jnp.broadcast_to(
        grad.astype(bf16)[None], (spread.shape[0],) + grad.shape
    )
    tail = total[:, width:]
    lane = lax.broadcasted_iota(jnp.int32, tail.shape, 1)
    loss = jnp.sum(jnp.where(lane < 2, tail, 0.0), axis=1, keepdims=True)
    high = loss.astype(bf16).astype(f32)
    low = loss - high
    tail = jnp.where(lane == 0, high, jnp.where(lane == 1, low, 0.0)).astype(bf16)
    spread[:, :, width:] = jnp.broadcast_to(tail[None], (spread.shape[0],) + tail.shape)


def body(pooled_feats, head_weight, text_embed, logit_scale, logit_bias):
    each, width = text_embed.shape
    rows, deep = pooled_feats.shape
    members = lax.axis_size("fsdp")
    chips = lax.axis_size("dp") // 2
    group_id = lax.axis_index("dp")
    member_id = lax.axis_index("fsdp")
    core = group_id % 2
    wide = width + 128

    part, text_spread = call(
        front_kernel,
        [((rows, width), f32), ((chips, each, width), bf16)],
        [VM] * 3,
        (pooled_feats, head_weight, text_embed),
    )
    with jax.named_scope("text_gather"):
        own = same_core(text_spread.reshape(chips * each, width))
        part, own = lax.optimization_barrier((part, own))
        other = swapped(own)
    with jax.named_scope("head_reduce"):
        parts = over_fsdp(part).reshape(members, each, width)
    hat, lengths, unit_spread = call(
        unit_kernel,
        [((each, width), f32), ((each, 128), f32), ((members, each, width), bf16)],
        [VM],
        (parts,),
    )
    with jax.named_scope("unit_gather"):
        units = over_fsdp(unit_spread.reshape(rows, width))
    image, text_own, text_other = call(
        pair_kernel,
        [((rows, wide), bf16), ((chips * each, width), f32), ((chips * each, width), bf16)],
        [SM, SM, VM, VM, VM],
        (
            jnp.concatenate([logit_scale, logit_bias]),
            jnp.stack([group_id // 2, member_id, jnp.int32(each)]).astype(jnp.int32),
            units,
            own,
            other,
        ),
    )
    with jax.named_scope("text_swap"):
        text_from = swapped(text_other)
    with jax.named_scope("image_reduce"):
        parts = over_fsdp(image).reshape(members, each, wide)
    (grad_spread,) = call(
        grad_kernel,
        [((members, each, wide), bf16)],
        [VM] * 3,
        (parts, hat, lengths),
    )
    with jax.named_scope("grad_gather"):
        grads = over_fsdp(grad_spread.reshape(rows, wide))
    unit_grad = grads[:, :width]
    losses = grads[:, width].astype(f32) + grads[:, width + 1].astype(f32)
    pooled_grad = lax.dot_general(
        unit_grad, head_weight, (((1,), (1,)), ((), ())), preferred_element_type=f32
    )
    head_part = lax.dot_general(
        unit_grad, pooled_feats, (((0,), (0,)), ((), ())), preferred_element_type=f32
    )
    cols = width // (2 * chips)
    head_part = head_part.reshape(chips, 2, cols, deep)
    mine = lax.dynamic_index_in_dim(head_part, core, 1, keepdims=False)
    away = lax.dynamic_index_in_dim(head_part, 1 - core, 1, keepdims=False)
    with jax.named_scope("head_swap"):
        mine = mine + swapped(away.astype(bf16)).astype(f32)
    mine = jnp.pad(mine.astype(bf16), ((0, 0), (0, 0), (0, 128 - deep)))
    mine = mine.reshape(chips, cols // 8, 8, 128)
    text_sum = (text_own + text_from.astype(f32)).astype(bf16)
    text_sum = text_sum.reshape(chips, each, width // 128, 128).transpose(0, 2, 1, 3)
    packed = jnp.concatenate([text_sum, mine], axis=1)
    blocks = packed.shape[1]
    with jax.named_scope("last_reduce"):
        packed = same_core(packed.reshape(chips * blocks, 8, 128)).reshape(chips, blocks, 8, 128)
    final = jnp.sum(packed.astype(f32), axis=0)
    text_grad = final[: width // 128].transpose(1, 0, 2).reshape(each, width)
    head_grad = final[width // 128 :].reshape(cols, 128)[:, :deep].T
    return (losses, head_grad, pooled_grad, text_grad)


def solution(mesh):
    return jax.shard_map(
        body,
        mesh=mesh,
        in_specs=(P("dp", "fsdp"), P("fsdp", None), P(("dp", "fsdp"), None), P(), P()),
        out_specs=(P("dp"), P("fsdp", "dp"), P("dp", "fsdp"), P(("dp", "fsdp"), None)),
        check_vma=False,
    )
```

```python
import functools

import jax
import jax.numpy as jnp
from jax import lax
from jax.experimental import pallas as pl
from jax.experimental.pallas import tpu as pltpu
from jax.sharding import PartitionSpec as P

epsilon = 1e-06
bf16 = jnp.bfloat16
f32 = jnp.float32
VM = pl.BlockSpec(memory_space=pltpu.VMEM)
SM = pl.BlockSpec(memory_space=pltpu.SMEM)
ALONG_Y = 8


def call(kernel, outs, in_specs, args, mib=8):
    return pl.pallas_call(
        kernel,
        out_shape=[jax.ShapeDtypeStruct(s, d) for s, d in outs],
        in_specs=in_specs,
        out_specs=[VM] * len(outs),
        compiler_params=pltpu.CompilerParams(vmem_limit_bytes=mib * 1024 * 1024),
    )(*args)


def passed(value, mask):
    count = lax.axis_size("dp")
    return lax.ppermute(value, "dp", [(s, s ^ mask) for s in range(count)])


def same_core(value):
    count = lax.axis_size("dp")
    groups = [list(range(c, count, 2)) for c in range(2)]
    return lax.all_to_all(value, "dp", 0, 0, axis_index_groups=groups, tiled=True)


def spread_over(value, step, count):
    return jnp.concatenate([value] + [passed(value, step * k) for k in range(1, count)], axis=0)


def summed_over(value, step, count):
    size = value.shape[0] // count
    total = value[:size]
    for k in range(1, count):
        block = value[k * size : (k + 1) * size].astype(bf16)
        total = total + passed(block, step * k).astype(f32)
    return total


def over_fsdp(value):
    return lax.all_to_all(value, "fsdp", 0, 0, tiled=True)


def text_kernel(text, unit):
    t = text[...].astype(f32)
    t = t / jnp.sqrt(jnp.sum(t * t, axis=1, keepdims=True) + epsilon)
    unit[...] = t.astype(bf16)


def head_kernel(feats, weight, part):
    part[...] = lax.dot_general(
        feats[...], weight[...], (((0,), (0,)), ((), ())), preferred_element_type=f32
    )


def unit_kernel(parts, hat, lengths, spread):
    raw = jnp.sum(parts[...].astype(f32), axis=0)
    size = jnp.sqrt(jnp.sum(raw * raw, axis=1, keepdims=True) + epsilon)
    value = raw / size
    hat[...] = value
    lengths[...] = jnp.broadcast_to(size, lengths.shape)
    spread[...] = jnp.broadcast_to(value.astype(bf16)[None], spread.shape)


def pair_kernel(scalars, where, units, own, other, image, text_own, text_other):
    width = units.shape[1]
    temper, offset = scalars[0], scalars[1]
    first, each = where[0], where[1]
    rows = units[...]
    total = None
    losses = None
    for half, (texts, out) in enumerate(((own, text_own), (other, text_other))):
        block = texts[...]
        scores = lax.dot_general(
            rows, block, (((1,), (1,)), ((), ())), preferred_element_type=f32
        )
        logits = temper * scores + offset
        if half == 0:
            row = lax.broadcasted_iota(jnp.int32, logits.shape, 0) - first
            col = lax.broadcasted_iota(jnp.int32, logits.shape, 1)
            positive = (row == col) & (col < each)
            sign = jnp.where(positive, -1.0, 1.0).astype(f32)
            logits = sign * logits
        small = jnp.exp(-jnp.abs(logits))
        loss = jnp.sum(jnp.maximum(logits, 0.0) + jnp.log1p(small), axis=1, keepdims=True)
        weights = jnp.where(logits >= 0, 1.0, small) / (1.0 + small) * temper
        if half == 0:
            weights = weights * sign
        weights = weights.astype(bf16)
        part = jnp.dot(weights, block, preferred_element_type=f32)
        out[...] = lax.dot_general(
            weights, rows, (((0,), (0,)), ((), ())), preferred_element_type=f32
        ).astype(out.dtype)
        total = part if half == 0 else total + part
        losses = loss if half == 0 else losses + loss
    image[:, :width] = total.astype(bf16)
    high = losses.astype(bf16).astype(f32)
    low = losses - high
    lane = lax.broadcasted_iota(jnp.int32, (rows.shape[0], 128), 1)
    image[:, width:] = jnp.where(lane == 0, high, jnp.where(lane == 1, low, 0.0)).astype(bf16)


def grad_kernel(parts, hat, lengths, spread):
    width = hat.shape[1]
    total = jnp.sum(parts[...].astype(f32), axis=0)
    direction = total[:, :width]
    value = hat[...]
    projected = jnp.sum(value * direction, axis=1, keepdims=True)
    grad = (direction - value * projected) / lengths[:, :1]
    spread[:, :, :width] = jnp.broadcast_to(
        grad.astype(bf16)[None], (spread.shape[0],) + grad.shape
    )
    tail = total[:, width:]
    lane = lax.broadcasted_iota(jnp.int32, tail.shape, 1)
    loss = jnp.sum(jnp.where(lane < 2, tail, 0.0), axis=1, keepdims=True)
    high = loss.astype(bf16).astype(f32)
    low = loss - high
    tail = jnp.where(lane == 0, high, jnp.where(lane == 1, low, 0.0)).astype(bf16)
    spread[:, :, width:] = jnp.broadcast_to(tail[None], (spread.shape[0],) + tail.shape)


def body(pooled_feats, head_weight, text_embed, logit_scale, logit_bias):
    each, width = text_embed.shape
    rows, deep = pooled_feats.shape
    members = lax.axis_size("fsdp")
    chips = lax.axis_size("dp") // 2
    along_x = chips // ALONG_Y
    core = lax.axis_index("dp") % 2
    member_id = lax.axis_index("fsdp")
    wide = width + 128

    (text_unit,) = call(text_kernel, [((each, width), bf16)], [VM], (text_embed,))
    with jax.named_scope("text_gather"):
        own = spread_over(text_unit, 2 * ALONG_Y, along_x)
        own = spread_over(own, 2, ALONG_Y)
        other = passed(own, 1)
    (part,) = call(head_kernel, [((rows, width), f32)], [VM] * 2, (pooled_feats.T, head_weight))
    with jax.named_scope("head_reduce"):
        parts = over_fsdp(part).reshape(members, each, width)
    hat, lengths, unit_spread = call(
        unit_kernel,
        [((each, width), f32), ((each, 128), f32), ((members, each, width), bf16)],
        [VM],
        (parts,),
    )
    with jax.named_scope("unit_gather"):
        units = over_fsdp(unit_spread.reshape(rows, width))
    image, text_own, text_other = call(
        pair_kernel,
        [((rows, wide), bf16), ((chips * each, width), f32), ((chips * each, width), bf16)],
        [SM, SM, VM, VM, VM],
        (
            jnp.concatenate([logit_scale, logit_bias]),
            jnp.stack([member_id * each, jnp.int32(each)]).astype(jnp.int32),
            units,
            own,
            other,
        ),
        mib=24,
    )
    with jax.named_scope("text_reduce"):
        text_sum = text_own + passed(text_other, 1).astype(f32)
        text_sum = summed_over(text_sum, 2, ALONG_Y)
        text_grad = summed_over(text_sum, 2 * ALONG_Y, along_x)
    with jax.named_scope("image_reduce"):
        parts = over_fsdp(image).reshape(members, each, wide)
    (grad_spread,) = call(
        grad_kernel,
        [((members, each, wide), bf16)],
        [VM] * 3,
        (parts, hat, lengths),
    )
    with jax.named_scope("grad_gather"):
        grads = over_fsdp(grad_spread.reshape(rows, wide))
    unit_grad = grads[:, :width]
    losses = grads[:, width].astype(f32) + grads[:, width + 1].astype(f32)
    pooled_grad = lax.dot_general(
        unit_grad, head_weight, (((1,), (1,)), ((), ())), preferred_element_type=f32
    )
    head_part = lax.dot_general(
        unit_grad, pooled_feats, (((0,), (0,)), ((), ())), preferred_element_type=f32
    )
    cols = width // (2 * chips)
    head_part = head_part.reshape(chips, 2, cols, deep)
    mine = lax.dynamic_index_in_dim(head_part, core, 1, keepdims=False)
    away = lax.dynamic_index_in_dim(head_part, 1 - core, 1, keepdims=False)
    with jax.named_scope("head_swap"):
        mine = mine + passed(away.astype(bf16), 1).astype(f32)
    with jax.named_scope("last_reduce"):
        mine = same_core(mine.astype(bf16))
    head_grad = jnp.sum(mine.astype(f32), axis=0).T
    return (losses, head_grad, pooled_grad, text_grad)


def solution(mesh):
    return jax.shard_map(
        body,
        mesh=mesh,
        in_specs=(P("dp", "fsdp"), P("fsdp", None), P(("dp", "fsdp"), None), P(), P()),
        out_specs=(P("dp"), P("fsdp", "dp"), P("dp", "fsdp"), P(("dp", "fsdp"), None)),
        check_vma=False,
    )
```

```python
import functools

import jax
import jax.numpy as jnp
from jax import lax
from jax.experimental import pallas as pl
from jax.experimental.pallas import tpu as pltpu
from jax.sharding import PartitionSpec as P

epsilon = 1e-06
bf16 = jnp.bfloat16
f32 = jnp.float32
VM = pl.BlockSpec(memory_space=pltpu.VMEM)
SM = pl.BlockSpec(memory_space=pltpu.SMEM)
FIRST = (32, 8, 4, 1)
LAST = (2, 16)


def call(kernel, outs, in_specs, args, mib=8):
    return pl.pallas_call(
        kernel,
        out_shape=[jax.ShapeDtypeStruct(s, d) for s, d in outs],
        in_specs=in_specs,
        out_specs=[VM] * len(outs),
        compiler_params=pltpu.CompilerParams(vmem_limit_bytes=mib * 1024 * 1024),
    )(*args)


def passed(value, mask):
    count = lax.axis_size("dp")
    return lax.ppermute(value, "dp", [(s, s ^ mask) for s in range(count)])


def same_core(value):
    count = lax.axis_size("dp")
    groups = [list(range(c, count, 2)) for c in range(2)]
    return lax.all_to_all(value, "dp", 0, 0, axis_index_groups=groups, tiled=True)


def spread_over(value, masks):
    for mask in masks:
        value = jnp.concatenate([value, passed(value, mask)], axis=0)
    return value


def halves_passed(value, mask):
    size = value.shape[0] // 2
    return value[:size], passed(value[size:].astype(bf16), mask)


def halves_added(pair):
    return pair[0] + pair[1].astype(f32)


def summed_over(value, masks):
    for mask in masks:
        value = halves_added(halves_passed(value, mask))
    return value


def over_fsdp(value):
    return lax.all_to_all(value, "fsdp", 0, 0, tiled=True)


def text_kernel(text, unit):
    t = text[...].astype(f32)
    t = t / jnp.sqrt(jnp.sum(t * t, axis=1, keepdims=True) + epsilon)
    unit[...] = t.astype(bf16)


def head_kernel(feats, weight, part):
    part[...] = lax.dot_general(
        feats[...], weight[...], (((0,), (0,)), ((), ())), preferred_element_type=f32
    )


def unit_kernel(parts, hat, lengths, spread):
    raw = jnp.sum(parts[...].astype(f32), axis=0)
    size = jnp.sqrt(jnp.sum(raw * raw, axis=1, keepdims=True) + epsilon)
    value = raw / size
    hat[...] = value
    lengths[...] = jnp.broadcast_to(size, lengths.shape)
    spread[...] = jnp.broadcast_to(value.astype(bf16)[None], spread.shape)


def pair_kernel(scalars, where, units, *blocks_and_outs):
    *blocks, image, spread = blocks_and_outs
    width = units.shape[1]
    temper, offset = scalars[0], scalars[1]
    first, each = where[0], where[1]
    rows = units[...]
    total = None
    losses = None
    for index, texts in enumerate(blocks):
        block = texts[...]
        scores = lax.dot_general(
            rows, block, (((1,), (1,)), ((), ())), preferred_element_type=f32
        )
        logits = temper * scores + offset
        if index == 0:
            row = lax.broadcasted_iota(jnp.int32, logits.shape, 0) - first
            col = lax.broadcasted_iota(jnp.int32, logits.shape, 1)
            positive = (row == col) & (col < each)
            sign = jnp.where(positive, -1.0, 1.0).astype(f32)
            logits = sign * logits
        small = jnp.exp(-jnp.abs(logits))
        loss = jnp.sum(jnp.maximum(logits, 0.0) + jnp.log1p(small), axis=1, keepdims=True)
        weights = jnp.where(logits >= 0, 1.0, small) / (1.0 + small) * temper
        if index == 0:
            weights = weights * sign
        weights = weights.astype(bf16)
        part = jnp.dot(weights, block, preferred_element_type=f32)
        spread[:, index * block.shape[0] : (index + 1) * block.shape[0]] = weights
        total = part if index == 0 else total + part
        losses = loss if index == 0 else losses + loss
    image[:, :width] = total.astype(bf16)
    high = losses.astype(bf16).astype(f32)
    low = losses - high
    lane = lax.broadcasted_iota(jnp.int32, (rows.shape[0], 128), 1)
    image[:, width:] = jnp.where(lane == 0, high, jnp.where(lane == 1, low, 0.0)).astype(bf16)


def turn_kernel(weights, units, own, other):
    rows = units[...]
    count = 4
    size = weights.shape[1] // count
    half = size // 2
    for index in range(count):
        block = lax.dot_general(
            weights[:, index * size : (index + 1) * size],
            rows,
            (((0,), (0,)), ((), ())),
            preferred_element_type=f32,
        )
        own[index * half : (index + 1) * half, :] = block[:half]
        other[index * half : (index + 1) * half, :] = block[half:].astype(bf16)


def grad_kernel(parts, hat, lengths, spread):
    width = hat.shape[1]
    total = jnp.sum(parts[...].astype(f32), axis=0)
    direction = total[:, :width]
    value = hat[...]
    projected = jnp.sum(value * direction, axis=1, keepdims=True)
    grad = (direction - value * projected) / lengths[:, :1]
    spread[:, :, :width] = jnp.broadcast_to(
        grad.astype(bf16)[None], (spread.shape[0],) + grad.shape
    )
    tail = total[:, width:]
    lane = lax.broadcasted_iota(jnp.int32, tail.shape, 1)
    loss = jnp.sum(jnp.where(lane < 2, tail, 0.0), axis=1, keepdims=True)
    high = loss.astype(bf16).astype(f32)
    low = loss - high
    tail = jnp.where(lane == 0, high, jnp.where(lane == 1, low, 0.0)).astype(bf16)
    spread[:, :, width:] = jnp.broadcast_to(tail[None], (spread.shape[0],) + tail.shape)


def body(pooled_feats, head_weight, text_embed, logit_scale, logit_bias):
    each, width = text_embed.shape
    rows, deep = pooled_feats.shape
    members = lax.axis_size("fsdp")
    chips = lax.axis_size("dp") // 2
    core = lax.axis_index("dp") % 2
    member_id = lax.axis_index("fsdp")
    wide = width + 128

    (text_unit,) = call(text_kernel, [((each, width), bf16)], [VM], (text_embed,))
    first = [mask for mask in FIRST if mask < 2 * chips]
    with jax.named_scope("text_gather"):
        block = spread_over(text_unit, first[:1])
        block, pooled_feats = lax.optimization_barrier((block, pooled_feats))
        block = spread_over(block, first[1:])
        blocks = [block] + [passed(block, mask) for mask in (LAST[0], LAST[1], sum(LAST))]
    (part,) = call(head_kernel, [((rows, width), f32)], [VM] * 2, (pooled_feats.T, head_weight))
    with jax.named_scope("head_reduce"):
        parts = over_fsdp(part).reshape(members, each, width)
    hat, lengths, unit_spread = call(
        unit_kernel,
        [((each, width), f32), ((each, 128), f32), ((members, each, width), bf16)],
        [VM],
        (parts,),
    )
    with jax.named_scope("unit_gather"):
        units = over_fsdp(unit_spread.reshape(rows, width))
    image, weights = call(
        pair_kernel,
        [((rows, wide), bf16), ((rows, 2 * chips * each), bf16)],
        [SM, SM, VM] + [VM] * len(blocks),
        (
            jnp.concatenate([logit_scale, logit_bias]),
            jnp.stack([member_id * each, jnp.int32(each)]).astype(jnp.int32),
            units,
            *blocks,
        ),
        mib=16,
    )
    text_own, text_other = call(
        turn_kernel,
        [((chips * each, width), f32), ((chips * each, width), bf16)],
        [VM, VM],
        (weights, units),
        mib=16,
    )
    masks = LAST[::-1] + tuple(first[-2::-1])
    with jax.named_scope("text_reduce"):
        text_sum = text_own + passed(text_other, 1).astype(f32)
        sent = halves_passed(text_sum, masks[0])
    with jax.named_scope("image_reduce"):
        parts = over_fsdp(image).reshape(members, each, wide)
    sent, parts = lax.optimization_barrier((sent, parts))
    with jax.named_scope("text_reduce"):
        text_sum = summed_over(halves_added(sent), masks[1:2])
        sent = halves_passed(text_sum, masks[2])
    (grad_spread,) = call(
        grad_kernel,
        [((members, each, wide), bf16)],
        [VM] * 3,
        (parts, hat, lengths),
    )
    with jax.named_scope("grad_gather"):
        grads = over_fsdp(grad_spread.reshape(rows, wide))
    sent, _ = lax.optimization_barrier((sent, grads))
    with jax.named_scope("text_reduce"):
        text_sum = summed_over(halves_added(sent), masks[3:-1])
        sent = halves_passed(text_sum, masks[-1])
    unit_grad = grads[:, :width]
    losses = grads[:, width].astype(f32) + grads[:, width + 1].astype(f32)
    head_part = lax.dot_general(
        unit_grad, pooled_feats, (((0,), (0,)), ((), ())), preferred_element_type=f32
    )
    cols = width // (2 * chips)
    head_part = head_part.reshape(chips, 2, cols, deep)
    mine = lax.dynamic_index_in_dim(head_part, core, 1, keepdims=False)
    away = lax.dynamic_index_in_dim(head_part, 1 - core, 1, keepdims=False)
    with jax.named_scope("head_swap"):
        mine = mine + passed(away.astype(bf16), 1).astype(f32)
    mine = mine.astype(bf16)
    unit_grad, mine = lax.optimization_barrier((unit_grad, mine))
    with jax.named_scope("last_reduce"):
        mine = same_core(mine)
    pooled_grad = lax.dot_general(
        unit_grad, head_weight, (((1,), (1,)), ((), ())), preferred_element_type=f32
    )
    sent, mine = lax.optimization_barrier((sent, mine))
    text_grad = halves_added(sent)
    head_grad = jnp.sum(mine.astype(f32), axis=0).T
    return (losses, head_grad, pooled_grad, text_grad)


def solution(mesh):
    return jax.shard_map(
        body,
        mesh=mesh,
        in_specs=(P("dp", "fsdp"), P("fsdp", None), P(("dp", "fsdp"), None), P(), P()),
        out_specs=(P("dp"), P("fsdp", "dp"), P("dp", "fsdp"), P(("dp", "fsdp"), None)),
        check_vma=False,
    )
```

```python
import functools

import jax
import jax.numpy as jnp
from jax import lax
from jax.experimental import pallas as pl
from jax.experimental.pallas import tpu as pltpu
from jax.sharding import PartitionSpec as P

epsilon = 1e-06
bf16 = jnp.bfloat16
f32 = jnp.float32
VM = pl.BlockSpec(memory_space=pltpu.VMEM)
SM = pl.BlockSpec(memory_space=pltpu.SMEM)
MASKS = (16, 2, 4, 8, 32)


def call(kernel, outs, in_specs, args, mib=8):
    return pl.pallas_call(
        kernel,
        out_shape=[jax.ShapeDtypeStruct(s, d) for s, d in outs],
        in_specs=in_specs,
        out_specs=[VM] * len(outs),
        compiler_params=pltpu.CompilerParams(vmem_limit_bytes=mib * 1024 * 1024),
    )(*args)


def passed(value, mask):
    count = lax.axis_size("dp")
    return lax.ppermute(value, "dp", [(s, s ^ mask) for s in range(count)])


def same_core():
    count = lax.axis_size("dp")
    return [list(range(c, count, 2)) for c in range(2)]


def halves_passed(value, mask):
    size = value.shape[0] // 2
    return value[:size], passed(value[size:].astype(bf16), mask)


def halves_added(pair):
    return pair[0] + pair[1].astype(f32)


def summed_over(value, masks):
    for mask in masks:
        value = halves_added(halves_passed(value, mask))
    return value


def over_fsdp(value):
    return lax.all_to_all(value, "fsdp", 0, 0, tiled=True)


def text_kernel(text, unit):
    t = text[...].astype(f32)
    t = t / jnp.sqrt(jnp.sum(t * t, axis=1, keepdims=True) + epsilon)
    unit[...] = t.astype(bf16)


def head_kernel(feats, weight, part):
    part[...] = lax.dot_general(
        feats[...], weight[...], (((0,), (0,)), ((), ())), preferred_element_type=f32
    )


def unit_kernel(parts, hat, lengths, spread):
    raw = jnp.sum(parts[...].astype(f32), axis=0)
    size = jnp.sqrt(jnp.sum(raw * raw, axis=1, keepdims=True) + epsilon)
    value = raw / size
    hat[...] = value
    lengths[...] = jnp.broadcast_to(size, lengths.shape)
    spread[...] = jnp.broadcast_to(value.astype(bf16)[None], spread.shape)


def order_of(masks):
    order = [0]
    for mask in masks[::-1]:
        order = order + [chip ^ (mask // 2) for chip in order]
    return order


def pair_kernel(order, scalars, where, units, texts, image, spread, block):
    width = units.shape[1]
    temper, offset = scalars[0], scalars[1]
    first, each, chip = where[0], where[1], where[2]
    size = block.shape[0] // len(order)
    for index, other in enumerate(order):
        source = pl.multiple_of((chip ^ other) * size, size)
        block[index * size : (index + 1) * size, :] = texts[pl.ds(source, size), :]
    rows = units[...]
    texts = block[...]
    scores = lax.dot_general(rows, texts, (((1,), (1,)), ((), ())), preferred_element_type=f32)
    row = lax.broadcasted_iota(jnp.int32, scores.shape, 0) - first
    col = lax.broadcasted_iota(jnp.int32, scores.shape, 1)
    sign = jnp.where((row == col) & (col < each), -1.0, 1.0).astype(f32)
    logits = sign * (temper * scores + offset)
    small = jnp.exp(-jnp.abs(logits))
    losses = jnp.sum(jnp.maximum(logits, 0.0) + jnp.log1p(small), axis=1, keepdims=True)
    weights = sign * (jnp.where(logits >= 0, 1.0, small) / (1.0 + small)) * temper
    weights = weights.astype(bf16)
    spread[...] = weights
    total = jnp.dot(weights, texts, preferred_element_type=f32)
    image[:, :width] = total.astype(bf16)
    high = losses.astype(bf16).astype(f32)
    low = losses - high
    lane = lax.broadcasted_iota(jnp.int32, (rows.shape[0], 128), 1)
    image[:, width:] = jnp.where(lane == 0, high, jnp.where(lane == 1, low, 0.0)).astype(bf16)


def turn_kernel(weights, units, own, other):
    block = lax.dot_general(
        weights[...], units[...], (((0,), (0,)), ((), ())), preferred_element_type=f32
    )
    count, width = own.shape
    block = block.reshape(count // 8, 2, 8, width)
    own[...] = block[:, 0].reshape(count, width)
    other[...] = block[:, 1].reshape(count, width).astype(bf16)


def grad_kernel(parts, hat, lengths, spread):
    width = hat.shape[1]
    total = jnp.sum(parts[...].astype(f32), axis=0)
    direction = total[:, :width]
    value = hat[...]
    projected = jnp.sum(value * direction, axis=1, keepdims=True)
    grad = (direction - value * projected) / lengths[:, :1]
    spread[:, :, :width] = jnp.broadcast_to(
        grad.astype(bf16)[None], (spread.shape[0],) + grad.shape
    )
    tail = total[:, width:]
    lane = lax.broadcasted_iota(jnp.int32, tail.shape, 1)
    loss = jnp.sum(jnp.where(lane < 2, tail, 0.0), axis=1, keepdims=True)
    high = loss.astype(bf16).astype(f32)
    low = loss - high
    tail = jnp.where(lane == 0, high, jnp.where(lane == 1, low, 0.0)).astype(bf16)
    spread[:, :, width:] = jnp.broadcast_to(tail[None], (spread.shape[0],) + tail.shape)


def body(pooled_feats, head_weight, text_embed, logit_scale, logit_bias):
    each, width = text_embed.shape
    rows, deep = pooled_feats.shape
    members = lax.axis_size("fsdp")
    chips = lax.axis_size("dp") // 2
    core = lax.axis_index("dp") % 2
    member_id = lax.axis_index("fsdp")
    wide = width + 128

    (text_unit,) = call(text_kernel, [((each, width), bf16)], [VM], (text_embed,))
    masks = [mask for mask in MASKS if mask < 2 * chips]
    with jax.named_scope("text_gather"):
        both = jnp.concatenate([text_unit, passed(text_unit, 1)], axis=0)
        texts = lax.all_gather(both, "dp", axis_index_groups=same_core(), axis=0, tiled=True)
    (part,) = call(head_kernel, [((rows, width), f32)], [VM] * 2, (pooled_feats.T, head_weight))
    with jax.named_scope("head_reduce"):
        parts = over_fsdp(part).reshape(members, each, width)
    hat, lengths, unit_spread = call(
        unit_kernel,
        [((each, width), f32), ((each, 128), f32), ((members, each, width), bf16)],
        [VM],
        (parts,),
    )
    with jax.named_scope("unit_gather"):
        units = over_fsdp(unit_spread.reshape(rows, width))
    image, weights = pl.pallas_call(
        functools.partial(pair_kernel, order_of(masks)),
        out_shape=[
            jax.ShapeDtypeStruct((rows, wide), bf16),
            jax.ShapeDtypeStruct((rows, 2 * chips * each), bf16),
        ],
        in_specs=[SM, SM, VM, VM],
        out_specs=[VM, VM],
        scratch_shapes=[pltpu.VMEM((2 * chips * each, width), bf16)],
        compiler_params=pltpu.CompilerParams(vmem_limit_bytes=16 * 1024 * 1024),
    )(
        jnp.concatenate([logit_scale, logit_bias]),
        jnp.stack([member_id * each, jnp.int32(each), lax.axis_index("dp") // 2]).astype(jnp.int32),
        units,
        texts,
    )
    text_own, text_other = call(
        turn_kernel,
        [((chips * each, width), f32), ((chips * each, width), bf16)],
        [VM, VM],
        (weights, units),
        mib=16,
    )
    with jax.named_scope("text_reduce"):
        text_sum = text_own + passed(text_other, 1).astype(f32)
        sent = halves_passed(text_sum, masks[0])
    with jax.named_scope("image_reduce"):
        parts = over_fsdp(image).reshape(members, each, wide)
    sent, parts = lax.optimization_barrier((sent, parts))
    with jax.named_scope("text_reduce"):
        text_sum = summed_over(halves_added(sent), masks[1:2])
        sent = halves_passed(text_sum, masks[2])
    (grad_spread,) = call(
        grad_kernel,
        [((members, each, wide), bf16)],
        [VM] * 3,
        (parts, hat, lengths),
    )
    with jax.named_scope("grad_gather"):
        grads = over_fsdp(grad_spread.reshape(rows, wide))
    sent, _ = lax.optimization_barrier((sent, grads))
    with jax.named_scope("text_reduce"):
        text_sum = summed_over(halves_added(sent), masks[3:-1])
        sent = halves_passed(text_sum, masks[-1])
    unit_grad = grads[:, :width]
    losses = grads[:, width].astype(f32) + grads[:, width + 1].astype(f32)
    head_part = lax.dot_general(
        unit_grad, pooled_feats, (((0,), (0,)), ((), ())), preferred_element_type=f32
    )
    cols = width // (2 * chips)
    head_part = head_part.reshape(chips, 2, cols, deep)
    mine = lax.dynamic_index_in_dim(head_part, core, 1, keepdims=False)
    away = lax.dynamic_index_in_dim(head_part, 1 - core, 1, keepdims=False)
    with jax.named_scope("head_swap"):
        mine = mine + passed(away.astype(bf16), 1).astype(f32)
    mine = mine.astype(bf16)
    unit_grad, mine = lax.optimization_barrier((unit_grad, mine))
    with jax.named_scope("last_reduce"):
        mine = lax.all_to_all(mine, "dp", 0, 0, axis_index_groups=same_core(), tiled=True)
    pooled_grad = lax.dot_general(
        unit_grad, head_weight, (((1,), (1,)), ((), ())), preferred_element_type=f32
    )
    sent, mine = lax.optimization_barrier((sent, mine))
    text_grad = halves_added(sent)
    head_grad = jnp.sum(mine.astype(f32), axis=0).T
    return (losses, head_grad, pooled_grad, text_grad)


def solution(mesh):
    return jax.shard_map(
        body,
        mesh=mesh,
        in_specs=(P("dp", "fsdp"), P("fsdp", None), P(("dp", "fsdp"), None), P(), P()),
        out_specs=(P("dp"), P("fsdp", "dp"), P("dp", "fsdp"), P(("dp", "fsdp"), None)),
        check_vma=False,
    )
```

```python
import jax
import jax.numpy as jnp
from jax import lax
from jax.experimental import pallas as pl
from jax.experimental.pallas import tpu as pltpu
from jax.sharding import PartitionSpec as P

epsilon = 1e-06
bf16 = jnp.bfloat16
f32 = jnp.float32
VM = pl.BlockSpec(memory_space=pltpu.VMEM)
SM = pl.BlockSpec(memory_space=pltpu.SMEM)
FAR, NEAR, CORE = 32, 16, 1
ALONG_Y = 8
Y_BITS = (1, 2, 4)


def call(kernel, outs, in_specs, args, mib=8):
    return pl.pallas_call(
        kernel,
        out_shape=[jax.ShapeDtypeStruct(s, d) for s, d in outs],
        in_specs=in_specs,
        out_specs=[VM] * len(outs),
        compiler_params=pltpu.CompilerParams(vmem_limit_bytes=mib * 1024 * 1024),
    )(*args)


def passed(value, mask):
    count = lax.axis_size("dp")
    return lax.ppermute(value, "dp", [(s, s ^ mask) for s in range(count)])


def same_core():
    count = lax.axis_size("dp")
    return [list(range(c, count, 2)) for c in range(2)]


def same_line():
    count = lax.axis_size("dp")
    line = 2 * ALONG_Y
    return [list(range(s + c, s + line, 2)) for s in range(0, count, line) for c in range(2)]


def joined(value, mask):
    return jnp.concatenate([value, passed(value, mask)], axis=0)


def halves_passed(value, mask):
    size = value.shape[0] // 2
    return value[:size], passed(value[size:].astype(bf16), mask)


def halves_added(pair):
    return pair[0] + pair[1].astype(f32)


def over_fsdp(value):
    return lax.all_to_all(value, "fsdp", 0, 0, tiled=True)


def text_kernel(text, unit):
    t = text[...].astype(f32)
    t = t / jnp.sqrt(jnp.sum(t * t, axis=1, keepdims=True) + epsilon)
    unit[...] = t.astype(bf16)


def head_kernel(feats, weight, part):
    part[...] = lax.dot_general(
        feats[...], weight[...], (((0,), (0,)), ((), ())), preferred_element_type=f32
    )


def unit_kernel(parts, hat, lengths, spread):
    raw = jnp.sum(parts[...].astype(f32), axis=0)
    size = jnp.sqrt(jnp.sum(raw * raw, axis=1, keepdims=True) + epsilon)
    value = raw / size
    hat[...] = value
    lengths[...] = jnp.broadcast_to(size, lengths.shape)
    spread[...] = jnp.broadcast_to(value.astype(bf16)[None], spread.shape)


def order_of():
    order = [0]
    for bit in Y_BITS[::-1]:
        order = order + [chip ^ bit for chip in order]
    return order


def pair_kernel(scalars, where, units, own, away, image, spread, block):
    width = units.shape[1]
    temper, offset = scalars[0], scalars[1]
    first, each, along = where[0], where[1], where[2]
    size = 2 * 8
    count = own.shape[0]
    order = order_of()
    for half, texts in enumerate((own, away)):
        for index in range(count // size):
            start, place = index // len(order) * len(order), index % len(order)
            source = pl.multiple_of((start + (along ^ order[place])) * size, size)
            target = half * count + index * size
            block[target : target + size, :] = texts[pl.ds(source, size), :]
    rows = units[...]
    texts = block[...]
    scores = lax.dot_general(rows, texts, (((1,), (1,)), ((), ())), preferred_element_type=f32)
    row = lax.broadcasted_iota(jnp.int32, scores.shape, 0) - first
    col = lax.broadcasted_iota(jnp.int32, scores.shape, 1)
    sign = jnp.where((row == col) & (col < each), -1.0, 1.0).astype(f32)
    logits = sign * (temper * scores + offset)
    small = jnp.exp(-jnp.abs(logits))
    losses = jnp.sum(jnp.maximum(logits, 0.0) + jnp.log1p(small), axis=1, keepdims=True)
    weights = sign * (jnp.where(logits >= 0, 1.0, small) / (1.0 + small)) * temper
    weights = weights.astype(bf16)
    spread[...] = weights
    total = jnp.dot(weights, texts, preferred_element_type=f32)
    image[:, :width] = total.astype(bf16)
    high = losses.astype(bf16).astype(f32)
    low = losses - high
    lane = lax.broadcasted_iota(jnp.int32, (rows.shape[0], 128), 1)
    image[:, width:] = jnp.where(lane == 0, high, jnp.where(lane == 1, low, 0.0)).astype(bf16)


def turn_kernel(weights, units, own, away):
    count = own.shape[0]
    for half, out in enumerate((own, away)):
        out[...] = lax.dot_general(
            weights[:, half * count : (half + 1) * count],
            units[...],
            (((0,), (0,)), ((), ())),
            preferred_element_type=f32,
        ).astype(out.dtype)


def grad_kernel(parts, hat, lengths, spread):
    width = hat.shape[1]
    total = jnp.sum(parts[...].astype(f32), axis=0)
    direction = total[:, :width]
    value = hat[...]
    projected = jnp.sum(value * direction, axis=1, keepdims=True)
    grad = (direction - value * projected) / lengths[:, :1]
    spread[:, :, :width] = jnp.broadcast_to(
        grad.astype(bf16)[None], (spread.shape[0],) + grad.shape
    )
    tail = total[:, width:]
    lane = lax.broadcasted_iota(jnp.int32, tail.shape, 1)
    loss = jnp.sum(jnp.where(lane < 2, tail, 0.0), axis=1, keepdims=True)
    high = loss.astype(bf16).astype(f32)
    low = loss - high
    tail = jnp.where(lane == 0, high, jnp.where(lane == 1, low, 0.0)).astype(bf16)
    spread[:, :, width:] = jnp.broadcast_to(tail[None], (spread.shape[0],) + tail.shape)


def body(pooled_feats, head_weight, text_embed, logit_scale, logit_bias):
    each, width = text_embed.shape
    rows, deep = pooled_feats.shape
    members = lax.axis_size("fsdp")
    chips = lax.axis_size("dp") // 2
    core = lax.axis_index("dp") % 2
    member_id = lax.axis_index("fsdp")
    wide = width + 128

    (text_unit,) = call(text_kernel, [((each, width), bf16)], [VM], (text_embed,))
    with jax.named_scope("text_gather"):
        own = joined(text_unit, FAR)
        own = jnp.broadcast_to(own[None], (ALONG_Y,) + own.shape).reshape(-1, width)
        own = lax.all_to_all(own, "dp", 0, 0, axis_index_groups=same_line(), tiled=True)
        own = joined(own, NEAR)
        away = passed(own, CORE)
    (part,) = call(head_kernel, [((rows, width), f32)], [VM] * 2, (pooled_feats.T, head_weight))
    with jax.named_scope("head_reduce"):
        parts = over_fsdp(part).reshape(members, each, width)
    hat, lengths, unit_spread = call(
        unit_kernel,
        [((each, width), f32), ((each, 128), f32), ((members, each, width), bf16)],
        [VM],
        (parts,),
    )
    with jax.named_scope("unit_gather"):
        units = over_fsdp(unit_spread.reshape(rows, width))
    image, weights = pl.pallas_call(
        pair_kernel,
        out_shape=[
            jax.ShapeDtypeStruct((rows, wide), bf16),
            jax.ShapeDtypeStruct((rows, 2 * chips * each), bf16),
        ],
        in_specs=[SM, SM, VM, VM, VM],
        out_specs=[VM, VM],
        scratch_shapes=[pltpu.VMEM((2 * chips * each, width), bf16)],
        compiler_params=pltpu.CompilerParams(vmem_limit_bytes=16 * 1024 * 1024),
    )(
        jnp.concatenate([logit_scale, logit_bias]),
        jnp.stack([member_id * each, jnp.int32(each), lax.axis_index("dp") // 2 % ALONG_Y]).astype(
            jnp.int32
        ),
        units,
        own,
        away,
    )
    text_own, text_away = call(
        turn_kernel,
        [((chips * each, width), f32), ((chips * each, width), bf16)],
        [VM, VM],
        (weights, units),
        mib=16,
    )
    near_y, mid_y, far_y = [2 * bit for bit in Y_BITS]
    with jax.named_scope("text_reduce"):
        text_sum = halves_added((text_own, passed(text_away, CORE)))
        size = text_sum.shape[0] // 4
        block = [text_sum[k * size : (k + 1) * size] for k in range(4)]
        sent = [block[0]] + [
            passed(piece.astype(bf16), mask)
            for piece, mask in zip(block[1:], (near_y, NEAR, NEAR + near_y))
        ]
    with jax.named_scope("image_reduce"):
        parts = over_fsdp(image).reshape(members, each, wide)
    (grad_spread,) = call(
        grad_kernel,
        [((members, each, wide), bf16)],
        [VM] * 3,
        (parts, hat, lengths),
    )
    sent, _ = lax.optimization_barrier((sent, grad_spread))
    with jax.named_scope("text_reduce"):
        text_sum = sent[0] + sum(piece.astype(f32) for piece in sent[1:])
        text_sum = halves_added(halves_passed(text_sum, mid_y))
        sent = halves_passed(text_sum, far_y)
    with jax.named_scope("grad_gather"):
        grads = over_fsdp(grad_spread.reshape(rows, wide))
    unit_grad = grads[:, :width]
    losses = grads[:, width].astype(f32) + grads[:, width + 1].astype(f32)
    head_part = lax.dot_general(
        unit_grad, pooled_feats, (((0,), (0,)), ((), ())), preferred_element_type=f32
    )
    cols = width // (2 * chips)
    head_part = head_part.reshape(chips, 2, cols, deep)
    mine = lax.dynamic_index_in_dim(head_part, core, 1, keepdims=False)
    away = lax.dynamic_index_in_dim(head_part, 1 - core, 1, keepdims=False)
    with jax.named_scope("head_swap"):
        mine = mine + passed(away.astype(bf16), 1).astype(f32)
    mine = mine.astype(bf16)
    sent, _ = lax.optimization_barrier((sent, mine))
    with jax.named_scope("text_reduce"):
        sent = halves_passed(halves_added(sent), FAR)
    unit_grad, mine = lax.optimization_barrier((unit_grad, mine))
    with jax.named_scope("last_reduce"):
        mine = lax.all_to_all(mine, "dp", 0, 0, axis_index_groups=same_core(), tiled=True)
    pooled_grad = lax.dot_general(
        unit_grad, head_weight, (((1,), (1,)), ((), ())), preferred_element_type=f32
    )
    sent, mine = lax.optimization_barrier((sent, mine))
    text_grad = halves_added(sent)
    head_grad = jnp.sum(mine.astype(f32), axis=0).T
    return (losses, head_grad, pooled_grad, text_grad)


def solution(mesh):
    return jax.shard_map(
        body,
        mesh=mesh,
        in_specs=(P("dp", "fsdp"), P("fsdp", None), P(("dp", "fsdp"), None), P(), P()),
        out_specs=(P("dp"), P("fsdp", "dp"), P("dp", "fsdp"), P(("dp", "fsdp"), None)),
        check_vma=False,
    )
```

```python
import jax
import jax.numpy as jnp
from jax import lax
from jax.experimental import pallas as pl
from jax.experimental.pallas import tpu as pltpu
from jax.sharding import PartitionSpec as P

epsilon = 1e-06
bf16 = jnp.bfloat16
f32 = jnp.float32
VM = pl.BlockSpec(memory_space=pltpu.VMEM)
SM = pl.BlockSpec(memory_space=pltpu.SMEM)
FAR, NEAR, CORE = 32, 16, 1
ALONG_Y = 8
Y_BITS = (1, 2, 4)


def call(kernel, outs, in_specs, args, mib=8):
    return pl.pallas_call(
        kernel,
        out_shape=[jax.ShapeDtypeStruct(s, d) for s, d in outs],
        in_specs=in_specs,
        out_specs=[VM] * len(outs),
        compiler_params=pltpu.CompilerParams(vmem_limit_bytes=mib * 1024 * 1024),
    )(*args)


def passed(value, mask):
    count = lax.axis_size("dp")
    return lax.ppermute(value, "dp", [(s, s ^ mask) for s in range(count)])


def same_core():
    count = lax.axis_size("dp")
    return [list(range(c, count, 2)) for c in range(2)]


def same_line():
    count = lax.axis_size("dp")
    line = 2 * ALONG_Y
    return [list(range(s + c, s + line, 2)) for s in range(0, count, line) for c in range(2)]


def joined(value, mask):
    return jnp.concatenate([value, passed(value, mask)], axis=0)


def halves_passed(value, mask):
    size = value.shape[0] // 2
    return value[:size], passed(value[size:].astype(bf16), mask)


def halves_added(pair):
    return pair[0] + pair[1].astype(f32)


def over_fsdp(value):
    return lax.all_to_all(value, "fsdp", 0, 0, tiled=True)


def text_kernel(text, unit):
    t = text[...].astype(f32)
    t = t / jnp.sqrt(jnp.sum(t * t, axis=1, keepdims=True) + epsilon)
    unit[...] = t.astype(bf16)


def head_kernel(feats, weight, part):
    part[...] = lax.dot_general(
        feats[...], weight[...], (((0,), (0,)), ((), ())), preferred_element_type=f32
    ).astype(bf16)


def unit_kernel(parts, hat, lengths, spread):
    raw = jnp.sum(parts[...].astype(f32), axis=0)
    size = jnp.sqrt(jnp.sum(raw * raw, axis=1, keepdims=True) + epsilon)
    value = raw / size
    hat[...] = value
    lengths[...] = jnp.broadcast_to(size, lengths.shape)
    spread[...] = jnp.broadcast_to(value.astype(bf16)[None], spread.shape)


def order_of():
    order = [0]
    for bit in Y_BITS[::-1]:
        order = order + [chip ^ bit for chip in order]
    return order


def pair_kernel(scalars, where, units, own, away, image, spread, block):
    width = units.shape[1]
    temper, offset = scalars[0], scalars[1]
    first, each, along = where[0], where[1], where[2]
    size = 2 * 8
    count = own.shape[0]
    order = order_of()
    for half, texts in enumerate((own, away)):
        for index in range(count // size):
            start, place = index // len(order) * len(order), index % len(order)
            source = pl.multiple_of((start + (along ^ order[place])) * size, size)
            target = half * count + index * size
            block[target : target + size, :] = texts[pl.ds(source, size), :]
    rows = units[...]
    texts = block[...]
    scores = lax.dot_general(rows, texts, (((1,), (1,)), ((), ())), preferred_element_type=f32)
    row = lax.broadcasted_iota(jnp.int32, scores.shape, 0) - first
    col = lax.broadcasted_iota(jnp.int32, scores.shape, 1)
    sign = jnp.where((row == col) & (col < each), -1.0, 1.0).astype(f32)
    logits = sign * (temper * scores + offset)
    small = jnp.exp(-jnp.abs(logits))
    losses = jnp.sum(jnp.maximum(logits, 0.0) + jnp.log1p(small), axis=1, keepdims=True)
    weights = sign * (jnp.where(logits >= 0, 1.0, small) / (1.0 + small)) * temper
    weights = weights.astype(bf16)
    spread[...] = weights
    total = jnp.dot(weights, texts, preferred_element_type=f32)
    image[:, :width] = total.astype(bf16)
    high = losses.astype(bf16).astype(f32)
    low = losses - high
    lane = lax.broadcasted_iota(jnp.int32, (rows.shape[0], 128), 1)
    image[:, width:] = jnp.where(lane == 0, high, jnp.where(lane == 1, low, 0.0)).astype(bf16)


def turn_kernel(weights, units, own, away):
    count = own.shape[0]
    for half, out in enumerate((own, away)):
        out[...] = lax.dot_general(
            weights[:, half * count : (half + 1) * count],
            units[...],
            (((0,), (0,)), ((), ())),
            preferred_element_type=f32,
        ).astype(out.dtype)


def grad_kernel(parts, hat, lengths, spread):
    width = hat.shape[1]
    total = jnp.sum(parts[...].astype(f32), axis=0)
    direction = total[:, :width]
    value = hat[...]
    projected = jnp.sum(value * direction, axis=1, keepdims=True)
    grad = (direction - value * projected) / lengths[:, :1]
    spread[:, :, :width] = jnp.broadcast_to(
        grad.astype(bf16)[None], (spread.shape[0],) + grad.shape
    )
    tail = total[:, width:]
    lane = lax.broadcasted_iota(jnp.int32, tail.shape, 1)
    loss = jnp.sum(jnp.where(lane < 2, tail, 0.0), axis=1, keepdims=True)
    high = loss.astype(bf16).astype(f32)
    low = loss - high
    tail = jnp.where(lane == 0, high, jnp.where(lane == 1, low, 0.0)).astype(bf16)
    spread[:, :, width:] = jnp.broadcast_to(tail[None], (spread.shape[0],) + tail.shape)


def body(pooled_feats, head_weight, text_embed, logit_scale, logit_bias):
    each, width = text_embed.shape
    rows, deep = pooled_feats.shape
    members = lax.axis_size("fsdp")
    chips = lax.axis_size("dp") // 2
    core = lax.axis_index("dp") % 2
    member_id = lax.axis_index("fsdp")
    wide = width + 128

    (text_unit,) = call(text_kernel, [((each, width), bf16)], [VM], (text_embed,))
    with jax.named_scope("text_gather"):
        own = joined(text_unit, FAR)
        own = jnp.broadcast_to(own[None], (ALONG_Y,) + own.shape).reshape(-1, width)
        own = lax.all_to_all(own, "dp", 0, 0, axis_index_groups=same_line(), tiled=True)
        own = joined(own, NEAR)
        away = passed(own, CORE)
    (part,) = call(head_kernel, [((rows, width), bf16)], [VM] * 2, (pooled_feats.T, head_weight))
    with jax.named_scope("head_reduce"):
        parts = over_fsdp(part).reshape(members, each, width)
    hat, lengths, unit_spread = call(
        unit_kernel,
        [((each, width), f32), ((each, 128), f32), ((members, each, width), bf16)],
        [VM],
        (parts,),
    )
    with jax.named_scope("unit_gather"):
        units = over_fsdp(unit_spread.reshape(rows, width))
    image, weights = pl.pallas_call(
        pair_kernel,
        out_shape=[
            jax.ShapeDtypeStruct((rows, wide), bf16),
            jax.ShapeDtypeStruct((rows, 2 * chips * each), bf16),
        ],
        in_specs=[SM, SM, VM, VM, VM],
        out_specs=[VM, VM],
        scratch_shapes=[pltpu.VMEM((2 * chips * each, width), bf16)],
        compiler_params=pltpu.CompilerParams(vmem_limit_bytes=16 * 1024 * 1024),
    )(
        jnp.concatenate([logit_scale, logit_bias]),
        jnp.stack([member_id * each, jnp.int32(each), lax.axis_index("dp") // 2 % ALONG_Y]).astype(
            jnp.int32
        ),
        units,
        own,
        away,
    )
    text_own, text_away = call(
        turn_kernel,
        [((chips * each, width), f32), ((chips * each, width), bf16)],
        [VM, VM],
        (weights, units),
        mib=16,
    )
    near_y, mid_y, far_y = [2 * bit for bit in Y_BITS]
    with jax.named_scope("text_reduce"):
        text_sum = halves_added((text_own, passed(text_away, CORE)))
        size = text_sum.shape[0] // 4
        block = [text_sum[k * size : (k + 1) * size] for k in range(4)]
        sent = [block[0]] + [
            passed(piece.astype(bf16), mask)
            for piece, mask in zip(block[1:], (near_y, NEAR, NEAR + near_y))
        ]
    with jax.named_scope("image_reduce"):
        parts = over_fsdp(image).reshape(members, each, wide)
    (grad_spread,) = call(
        grad_kernel,
        [((members, each, wide), bf16)],
        [VM] * 3,
        (parts, hat, lengths),
    )
    sent, _ = lax.optimization_barrier((sent, grad_spread))
    with jax.named_scope("text_reduce"):
        text_sum = sent[0] + sum(piece.astype(f32) for piece in sent[1:])
        text_sum = halves_added(halves_passed(text_sum, mid_y))
        sent = halves_passed(text_sum, far_y)
    with jax.named_scope("grad_gather"):
        grads = over_fsdp(grad_spread.reshape(rows, wide))
    unit_grad = grads[:, :width]
    losses = grads[:, width].astype(f32) + grads[:, width + 1].astype(f32)
    head_part = lax.dot_general(
        unit_grad, pooled_feats, (((0,), (0,)), ((), ())), preferred_element_type=f32
    )
    cols = width // (2 * chips)
    head_part = head_part.reshape(chips, 2, cols, deep)
    mine = lax.dynamic_index_in_dim(head_part, core, 1, keepdims=False)
    away = lax.dynamic_index_in_dim(head_part, 1 - core, 1, keepdims=False)
    with jax.named_scope("head_swap"):
        mine = mine + passed(away.astype(bf16), 1).astype(f32)
    mine = mine.astype(bf16)
    sent, _ = lax.optimization_barrier((sent, mine))
    with jax.named_scope("text_reduce"):
        sent = halves_passed(halves_added(sent), FAR)
    unit_grad, mine = lax.optimization_barrier((unit_grad, mine))
    with jax.named_scope("last_reduce"):
        mine = lax.all_to_all(mine, "dp", 0, 0, axis_index_groups=same_core(), tiled=True)
    pooled_grad = lax.dot_general(
        unit_grad, head_weight, (((1,), (1,)), ((), ())), preferred_element_type=f32
    )
    sent, mine = lax.optimization_barrier((sent, mine))
    text_grad = halves_added(sent)
    head_grad = jnp.sum(mine.astype(f32), axis=0).T
    return (losses, head_grad, pooled_grad, text_grad)


def solution(mesh):
    return jax.shard_map(
        body,
        mesh=mesh,
        in_specs=(P("dp", "fsdp"), P("fsdp", None), P(("dp", "fsdp"), None), P(), P()),
        out_specs=(P("dp"), P("fsdp", "dp"), P("dp", "fsdp"), P(("dp", "fsdp"), None)),
        check_vma=False,
    )
```

```python
import jax
import jax.numpy as jnp
from jax import lax
from jax.experimental import pallas as pl
from jax.experimental.pallas import tpu as pltpu
from jax.sharding import PartitionSpec as P

epsilon = 1e-06
bf16 = jnp.bfloat16
f32 = jnp.float32
VM = pl.BlockSpec(memory_space=pltpu.VMEM)
SM = pl.BlockSpec(memory_space=pltpu.SMEM)
GATHER = (32, 16, 8, 4, 2)
REDUCE = (16, 2, 4, 8, 32)
CORE = 1


def call(kernel, outs, in_specs, args, mib=8):
    return pl.pallas_call(
        kernel,
        out_shape=[jax.ShapeDtypeStruct(s, d) for s, d in outs],
        in_specs=in_specs,
        out_specs=[VM] * len(outs),
        compiler_params=pltpu.CompilerParams(vmem_limit_bytes=mib * 1024 * 1024),
    )(*args)


def passed(value, mask):
    count = lax.axis_size("dp")
    return lax.ppermute(value, "dp", [(s, s ^ mask) for s in range(count)])


def same_core():
    count = lax.axis_size("dp")
    return [list(range(c, count, 2)) for c in range(2)]


def joined(value, mask):
    return jnp.concatenate([value, passed(value, mask)], axis=0)


def halves_passed(value, mask):
    size = value.shape[0] // 2
    return value[:size], passed(value[size:].astype(bf16), mask)


def halves_added(pair):
    return pair[0] + pair[1].astype(f32)


def over_fsdp(value):
    return lax.all_to_all(value, "fsdp", 0, 0, tiled=True)


def text_kernel(text, unit):
    t = text[...].astype(f32)
    t = t / jnp.sqrt(jnp.sum(t * t, axis=1, keepdims=True) + epsilon)
    unit[...] = t.astype(bf16)


def head_kernel(feats, weight, part):
    part[...] = lax.dot_general(
        feats[...], weight[...], (((0,), (0,)), ((), ())), preferred_element_type=f32
    ).astype(bf16)


def unit_kernel(parts, hat, lengths, spread):
    raw = jnp.sum(parts[...].astype(f32), axis=0)
    size = jnp.sqrt(jnp.sum(raw * raw, axis=1, keepdims=True) + epsilon)
    value = raw / size
    hat[...] = value
    lengths[...] = jnp.broadcast_to(size, lengths.shape)
    spread[...] = jnp.broadcast_to(value.astype(bf16)[None], spread.shape)


def place_of(index):
    bits = len(REDUCE)
    masks = [mask for bit, mask in enumerate(REDUCE) if index >> (bits - 1 - bit) & 1]
    return sum(1 << GATHER.index(mask) for mask in masks)


def pair_kernel(scalars, where, units, own, own_y, away, away_y, image, spread, block):
    width = units.shape[1]
    temper, offset = scalars[0], scalars[1]
    first, each = where[0], where[1]
    count = own.shape[0]
    size = 4 * count >> len(REDUCE)
    for half, pair in enumerate(((own, own_y), (away, away_y))):
        for index in range(2 * count // size):
            part, piece = divmod(place_of(2 * index) // 2, count // size)
            target = half * 2 * count + index * size
            block[target : target + size, :] = pair[part][piece * size : (piece + 1) * size, :]
    rows = units[...]
    texts = block[...]
    scores = lax.dot_general(rows, texts, (((1,), (1,)), ((), ())), preferred_element_type=f32)
    row = lax.broadcasted_iota(jnp.int32, scores.shape, 0) - first
    col = lax.broadcasted_iota(jnp.int32, scores.shape, 1)
    sign = jnp.where((row == col) & (col < each), -1.0, 1.0).astype(f32)
    logits = sign * (temper * scores + offset)
    small = jnp.exp(-jnp.abs(logits))
    losses = jnp.sum(jnp.maximum(logits, 0.0) + jnp.log1p(small), axis=1, keepdims=True)
    weights = sign * (jnp.where(logits >= 0, 1.0, small) / (1.0 + small)) * temper
    weights = weights.astype(bf16)
    spread[...] = weights
    total = jnp.dot(weights, texts, preferred_element_type=f32)
    image[:, :width] = total.astype(bf16)
    high = losses.astype(bf16).astype(f32)
    low = losses - high
    lane = lax.broadcasted_iota(jnp.int32, (rows.shape[0], 128), 1)
    image[:, width:] = jnp.where(lane == 0, high, jnp.where(lane == 1, low, 0.0)).astype(bf16)


def turn_kernel(weights, units, own, away):
    count = own.shape[0]
    for half, out in enumerate((own, away)):
        out[...] = lax.dot_general(
            weights[:, half * count : (half + 1) * count],
            units[...],
            (((0,), (0,)), ((), ())),
            preferred_element_type=f32,
        ).astype(out.dtype)


def grad_kernel(parts, hat, lengths, spread):
    width = hat.shape[1]
    total = jnp.sum(parts[...].astype(f32), axis=0)
    direction = total[:, :width]
    value = hat[...]
    projected = jnp.sum(value * direction, axis=1, keepdims=True)
    grad = (direction - value * projected) / lengths[:, :1]
    spread[:, :, :width] = jnp.broadcast_to(
        grad.astype(bf16)[None], (spread.shape[0],) + grad.shape
    )
    tail = total[:, width:]
    lane = lax.broadcasted_iota(jnp.int32, tail.shape, 1)
    loss = jnp.sum(jnp.where(lane < 2, tail, 0.0), axis=1, keepdims=True)
    high = loss.astype(bf16).astype(f32)
    low = loss - high
    tail = jnp.where(lane == 0, high, jnp.where(lane == 1, low, 0.0)).astype(bf16)
    spread[:, :, width:] = jnp.broadcast_to(tail[None], (spread.shape[0],) + tail.shape)


def body(pooled_feats, head_weight, text_embed, logit_scale, logit_bias):
    each, width = text_embed.shape
    rows, deep = pooled_feats.shape
    members = lax.axis_size("fsdp")
    chips = lax.axis_size("dp") // 2
    core = lax.axis_index("dp") % 2
    member_id = lax.axis_index("fsdp")
    wide = width + 128

    (text_unit,) = call(text_kernel, [((each, width), bf16)], [VM], (text_embed,))
    with jax.named_scope("text_gather"):
        own = joined(text_unit, GATHER[0])
        own, pooled_feats = lax.optimization_barrier((own, pooled_feats))
        for mask in GATHER[1:4]:
            own = joined(own, mask)
        last = GATHER[4]
        blocks = [own] + [passed(own, mask) for mask in (last, CORE, last + CORE)]
    (part,) = call(head_kernel, [((rows, width), bf16)], [VM] * 2, (pooled_feats.T, head_weight))
    with jax.named_scope("head_reduce"):
        parts = over_fsdp(part).reshape(members, each, width)
    hat, lengths, unit_spread = call(
        unit_kernel,
        [((each, width), f32), ((each, 128), f32), ((members, each, width), bf16)],
        [VM],
        (parts,),
    )
    with jax.named_scope("unit_gather"):
        units = over_fsdp(unit_spread.reshape(rows, width))
    image, weights = pl.pallas_call(
        pair_kernel,
        out_shape=[
            jax.ShapeDtypeStruct((rows, wide), bf16),
            jax.ShapeDtypeStruct((rows, 2 * chips * each), bf16),
        ],
        in_specs=[SM, SM] + [VM] * 5,
        out_specs=[VM, VM],
        scratch_shapes=[pltpu.VMEM((2 * chips * each, width), bf16)],
        compiler_params=pltpu.CompilerParams(vmem_limit_bytes=16 * 1024 * 1024),
    )(
        jnp.concatenate([logit_scale, logit_bias]),
        jnp.stack([member_id * each, jnp.int32(each)]).astype(jnp.int32),
        units,
        *blocks,
    )
    text_own, text_away = call(
        turn_kernel,
        [((chips * each, width), f32), ((chips * each, width), bf16)],
        [VM, VM],
        (weights, units),
        mib=16,
    )
    with jax.named_scope("text_reduce"):
        text_sum = halves_added((text_own, passed(text_away, CORE)))
        size = text_sum.shape[0] // 4
        block = [text_sum[k * size : (k + 1) * size] for k in range(4)]
        sent = [block[0]] + [
            passed(piece.astype(bf16), mask)
            for piece, mask in zip(block[1:], (REDUCE[1], REDUCE[0], REDUCE[0] + REDUCE[1]))
        ]
    with jax.named_scope("image_reduce"):
        parts = over_fsdp(image).reshape(members, each, wide)
    (grad_spread,) = call(
        grad_kernel,
        [((members, each, wide), bf16)],
        [VM] * 3,
        (parts, hat, lengths),
    )
    sent, _ = lax.optimization_barrier((sent, grad_spread))
    with jax.named_scope("text_reduce"):
        text_sum = sent[0] + sum(piece.astype(f32) for piece in sent[1:])
        text_sum = halves_added(halves_passed(text_sum, REDUCE[2]))
        sent = halves_passed(text_sum, REDUCE[3])
    with jax.named_scope("grad_gather"):
        grads = over_fsdp(grad_spread.reshape(rows, wide))
    unit_grad = grads[:, :width]
    losses = grads[:, width].astype(f32) + grads[:, width + 1].astype(f32)
    head_part = lax.dot_general(
        unit_grad, pooled_feats, (((0,), (0,)), ((), ())), preferred_element_type=f32
    )
    cols = width // (2 * chips)
    head_part = head_part.reshape(chips, 2, cols, deep)
    mine = lax.dynamic_index_in_dim(head_part, core, 1, keepdims=False)
    away = lax.dynamic_index_in_dim(head_part, 1 - core, 1, keepdims=False)
    with jax.named_scope("head_swap"):
        mine = mine + passed(away.astype(bf16), 1).astype(f32)
    mine = mine.astype(bf16)
    sent, _ = lax.optimization_barrier((sent, mine))
    with jax.named_scope("text_reduce"):
        sent = halves_passed(halves_added(sent), REDUCE[4])
    unit_grad, mine = lax.optimization_barrier((unit_grad, mine))
    with jax.named_scope("last_reduce"):
        mine = lax.all_to_all(mine, "dp", 0, 0, axis_index_groups=same_core(), tiled=True)
    pooled_grad = lax.dot_general(
        unit_grad, head_weight, (((1,), (1,)), ((), ())), preferred_element_type=f32
    )
    sent, mine = lax.optimization_barrier((sent, mine))
    text_grad = halves_added(sent)
    head_grad = jnp.sum(mine.astype(f32), axis=0).T
    return (losses, head_grad, pooled_grad, text_grad)


def solution(mesh):
    return jax.shard_map(
        body,
        mesh=mesh,
        in_specs=(P("dp", "fsdp"), P("fsdp", None), P(("dp", "fsdp"), None), P(), P()),
        out_specs=(P("dp"), P("fsdp", "dp"), P("dp", "fsdp"), P(("dp", "fsdp"), None)),
        check_vma=False,
    )
```

```python
import jax
import jax.numpy as jnp
from jax import lax
from jax.experimental import pallas as pl
from jax.experimental.pallas import tpu as pltpu
from jax.sharding import PartitionSpec as P

epsilon = 1e-06
bf16 = jnp.bfloat16
f32 = jnp.float32
VM = pl.BlockSpec(memory_space=pltpu.VMEM)
SM = pl.BlockSpec(memory_space=pltpu.SMEM)
GATHER = (32, 16, 8, 4, 2)
REDUCE = (16, 2, 4, 8, 32)
CORE = 1
HALVES = 2


def call(kernel, outs, in_specs, args, mib=8):
    return pl.pallas_call(
        kernel,
        out_shape=[jax.ShapeDtypeStruct(s, d) for s, d in outs],
        in_specs=in_specs,
        out_specs=[VM] * len(outs),
        compiler_params=pltpu.CompilerParams(vmem_limit_bytes=mib * 1024 * 1024),
    )(*args)


def passed(value, mask):
    count = lax.axis_size("dp")
    return lax.ppermute(value, "dp", [(s, s ^ mask) for s in range(count)])


def same_core():
    count = lax.axis_size("dp")
    return [list(range(c, count, 2)) for c in range(2)]


def joined(value, mask):
    return jnp.concatenate([value, passed(value, mask)], axis=0)


def halves_passed(value, mask):
    size = value.shape[0] // 2
    return value[:size], passed(value[size:].astype(bf16), mask)


def halves_added(pair):
    return pair[0] + pair[1].astype(f32)


def over_z(value):
    count = lax.axis_size("fsdp") // HALVES
    groups = [list(range(s * count, (s + 1) * count)) for s in range(HALVES)]
    return lax.all_to_all(value, "fsdp", 0, 0, axis_index_groups=groups, tiled=True)


def other_half(value):
    count = lax.axis_size("fsdp")
    return lax.ppermute(value, "fsdp", [(s, (s + count // 2) % count) for s in range(count)])


def text_kernel(text, unit):
    t = text[...].astype(f32)
    t = t / jnp.sqrt(jnp.sum(t * t, axis=1, keepdims=True) + epsilon)
    unit[...] = t.astype(bf16)


def head_kernel(feats, weight, part):
    rows = lax.dot_general(
        feats[...], weight[...], (((0,), (0,)), ((), ())), preferred_element_type=f32
    )
    count = rows.shape[0] // 8
    along = count // HALVES
    order = [half * along + z for z in range(along) for half in range(HALVES)]
    rows = jnp.concatenate([rows[8 * k : 8 * k + 8] for k in order], axis=0)
    part[...] = rows.astype(bf16)


def sum_kernel(parts, total):
    total[...] = jnp.sum(parts[...].astype(f32), axis=0)


def unit_kernel(mine, theirs, hat, lengths, spread):
    raw = mine[...] + theirs[...]
    size = jnp.sqrt(jnp.sum(raw * raw, axis=1, keepdims=True) + epsilon)
    value = raw / size
    hat[...] = value
    lengths[...] = jnp.broadcast_to(size, lengths.shape)
    spread[...] = jnp.broadcast_to(value.astype(bf16)[None], spread.shape)


def place_of(index):
    bits = len(REDUCE)
    masks = [mask for bit, mask in enumerate(REDUCE) if index >> (bits - 1 - bit) & 1]
    return sum(1 << GATHER.index(mask) for mask in masks)


def pair_kernel(scalars, where, units, own, own_y, away, away_y, image, spread, block):
    width = units.shape[1]
    temper, offset = scalars[0], scalars[1]
    first, each = where[0], where[1]
    count = own.shape[0]
    size = 4 * count >> len(REDUCE)
    for half, pair in enumerate(((own, own_y), (away, away_y))):
        for index in range(2 * count // size):
            part, piece = divmod(place_of(2 * index) // 2, count // size)
            target = half * 2 * count + index * size
            block[target : target + size, :] = pair[part][piece * size : (piece + 1) * size, :]
    rows = units[...]
    texts = block[...]
    scores = lax.dot_general(rows, texts, (((1,), (1,)), ((), ())), preferred_element_type=f32)
    row = lax.broadcasted_iota(jnp.int32, scores.shape, 0) - first
    col = lax.broadcasted_iota(jnp.int32, scores.shape, 1)
    sign = jnp.where((row == col) & (col < each), -1.0, 1.0).astype(f32)
    logits = sign * (temper * scores + offset)
    small = jnp.exp(-jnp.abs(logits))
    losses = jnp.sum(jnp.maximum(logits, 0.0) + jnp.log1p(small), axis=1, keepdims=True)
    weights = sign * (jnp.where(logits >= 0, 1.0, small) / (1.0 + small)) * temper
    weights = weights.astype(bf16)
    spread[...] = weights
    total = jnp.dot(weights, texts, preferred_element_type=f32)
    image[:, :width] = total.astype(bf16)
    high = losses.astype(bf16).astype(f32)
    low = losses - high
    lane = lax.broadcasted_iota(jnp.int32, (rows.shape[0], 128), 1)
    image[:, width:] = jnp.where(lane == 0, high, jnp.where(lane == 1, low, 0.0)).astype(bf16)


def turn_kernel(weights, units, own, away):
    count = own.shape[0]
    for half, out in enumerate((own, away)):
        out[...] = lax.dot_general(
            weights[:, half * count : (half + 1) * count],
            units[...],
            (((0,), (0,)), ((), ())),
            preferred_element_type=f32,
        ).astype(out.dtype)


def grad_kernel(mine, theirs, hat, lengths, spread):
    width = hat.shape[1]
    total = mine[...] + theirs[...]
    direction = total[:, :width]
    value = hat[...]
    projected = jnp.sum(value * direction, axis=1, keepdims=True)
    grad = (direction - value * projected) / lengths[:, :1]
    spread[:, :, :width] = jnp.broadcast_to(
        grad.astype(bf16)[None], (spread.shape[0],) + grad.shape
    )
    tail = total[:, width:]
    lane = lax.broadcasted_iota(jnp.int32, tail.shape, 1)
    loss = jnp.sum(jnp.where(lane < 2, tail, 0.0), axis=1, keepdims=True)
    high = loss.astype(bf16).astype(f32)
    low = loss - high
    tail = jnp.where(lane == 0, high, jnp.where(lane == 1, low, 0.0)).astype(bf16)
    spread[:, :, width:] = jnp.broadcast_to(tail[None], (spread.shape[0],) + tail.shape)


def body(pooled_feats, head_weight, text_embed, logit_scale, logit_bias):
    each, width = text_embed.shape
    rows, deep = pooled_feats.shape
    members = lax.axis_size("fsdp")
    chips = lax.axis_size("dp") // 2
    core = lax.axis_index("dp") % 2
    member_id = lax.axis_index("fsdp")
    along, both = members // HALVES, HALVES * each
    first = (member_id % along * HALVES + member_id // along) * each
    wide = width + 128

    (text_unit,) = call(text_kernel, [((each, width), bf16)], [VM], (text_embed,))
    with jax.named_scope("text_gather"):
        own = joined(text_unit, GATHER[0])
        own, pooled_feats = lax.optimization_barrier((own, pooled_feats))
        for mask in GATHER[1:4]:
            own = joined(own, mask)
        last = GATHER[4]
        blocks = [own] + [passed(own, mask) for mask in (last, CORE, last + CORE)]
    (part,) = call(head_kernel, [((rows, width), bf16)], [VM] * 2, (pooled_feats.T, head_weight))
    with jax.named_scope("head_reduce"):
        parts = over_z(part).reshape(along, both, width)
        (mine,) = call(sum_kernel, [((both, width), f32)], [VM], (parts,))
        theirs = other_half(mine)
    hat, lengths, unit_spread = call(
        unit_kernel,
        [((both, width), f32), ((both, 128), f32), ((along, both, width), bf16)],
        [VM] * 2,
        (mine, theirs),
    )
    with jax.named_scope("unit_gather"):
        units = over_z(unit_spread.reshape(rows, width))
    image, weights = pl.pallas_call(
        pair_kernel,
        out_shape=[
            jax.ShapeDtypeStruct((rows, wide), bf16),
            jax.ShapeDtypeStruct((rows, 2 * chips * each), bf16),
        ],
        in_specs=[SM, SM] + [VM] * 5,
        out_specs=[VM, VM],
        scratch_shapes=[pltpu.VMEM((2 * chips * each, width), bf16)],
        compiler_params=pltpu.CompilerParams(vmem_limit_bytes=16 * 1024 * 1024),
    )(
        jnp.concatenate([logit_scale, logit_bias]),
        jnp.stack([first, jnp.int32(each)]).astype(jnp.int32),
        units,
        *blocks,
    )
    text_own, text_away = call(
        turn_kernel,
        [((chips * each, width), f32), ((chips * each, width), bf16)],
        [VM, VM],
        (weights, units),
        mib=16,
    )
    with jax.named_scope("text_reduce"):
        text_sum = halves_added((text_own, passed(text_away, CORE)))
        size = text_sum.shape[0] // 4
        block = [text_sum[k * size : (k + 1) * size] for k in range(4)]
        sent = [block[0]] + [
            passed(piece.astype(bf16), mask)
            for piece, mask in zip(block[1:], (REDUCE[1], REDUCE[0], REDUCE[0] + REDUCE[1]))
        ]
    with jax.named_scope("image_reduce"):
        parts = over_z(image).reshape(along, both, wide)
        (mine,) = call(sum_kernel, [((both, wide), f32)], [VM], (parts,))
        theirs = other_half(mine)
    (grad_spread,) = call(
        grad_kernel,
        [((along, both, wide), bf16)],
        [VM] * 4,
        (mine, theirs, hat, lengths),
    )
    sent, _ = lax.optimization_barrier((sent, grad_spread))
    with jax.named_scope("text_reduce"):
        text_sum = sent[0] + sum(piece.astype(f32) for piece in sent[1:])
        text_sum = halves_added(halves_passed(text_sum, REDUCE[2]))
        sent = halves_passed(text_sum, REDUCE[3])
    with jax.named_scope("grad_gather"):
        grads = over_z(grad_spread.reshape(rows, wide))
    unit_grad = grads[:, :width]
    losses = grads[:, width].astype(f32) + grads[:, width + 1].astype(f32)
    by_z = pooled_feats.reshape(HALVES, along, each, deep).swapaxes(0, 1).reshape(rows, deep)
    head_part = lax.dot_general(
        unit_grad, by_z, (((0,), (0,)), ((), ())), preferred_element_type=f32
    )
    cols = width // (2 * chips)
    head_part = head_part.reshape(chips, 2, cols, deep)
    mine = lax.dynamic_index_in_dim(head_part, core, 1, keepdims=False)
    away = lax.dynamic_index_in_dim(head_part, 1 - core, 1, keepdims=False)
    with jax.named_scope("head_swap"):
        mine = mine + passed(away.astype(bf16), 1).astype(f32)
    mine = mine.astype(bf16)
    sent, _ = lax.optimization_barrier((sent, mine))
    with jax.named_scope("text_reduce"):
        sent = halves_passed(halves_added(sent), REDUCE[4])
    unit_grad, mine = lax.optimization_barrier((unit_grad, mine))
    with jax.named_scope("last_reduce"):
        mine = lax.all_to_all(mine, "dp", 0, 0, axis_index_groups=same_core(), tiled=True)
    pooled_grad = lax.dot_general(
        unit_grad, head_weight, (((1,), (1,)), ((), ())), preferred_element_type=f32
    )
    sent, mine = lax.optimization_barrier((sent, mine))
    text_grad = halves_added(sent)
    head_grad = jnp.sum(mine.astype(f32), axis=0).T
    losses = losses.reshape(along, HALVES, each).swapaxes(0, 1).reshape(rows)
    pooled_grad = pooled_grad.reshape(along, HALVES, each, deep).swapaxes(0, 1).reshape(rows, deep)
    return (losses, head_grad, pooled_grad, text_grad)


def solution(mesh):
    return jax.shard_map(
        body,
        mesh=mesh,
        in_specs=(P("dp", "fsdp"), P("fsdp", None), P(("dp", "fsdp"), None), P(), P()),
        out_specs=(P("dp"), P("fsdp", "dp"), P("dp", "fsdp"), P(("dp", "fsdp"), None)),
        check_vma=False,
    )
```

```python
import jax
import jax.numpy as jnp
from jax import lax
from jax.experimental import pallas as pl
from jax.experimental.pallas import tpu as pltpu
from jax.sharding import PartitionSpec as P

epsilon = 1e-06
bf16 = jnp.bfloat16
f32 = jnp.float32
VM = pl.BlockSpec(memory_space=pltpu.VMEM)
SM = pl.BlockSpec(memory_space=pltpu.SMEM)
GATHER = (32, 16, 8, 4, 2)
REDUCE = (16, 2, 4, 8, 32)
CORE = 1
HALVES = 2


def call(kernel, outs, in_specs, args, mib=8):
    return pl.pallas_call(
        kernel,
        out_shape=[jax.ShapeDtypeStruct(s, d) for s, d in outs],
        in_specs=in_specs,
        out_specs=[VM] * len(outs),
        compiler_params=pltpu.CompilerParams(vmem_limit_bytes=mib * 1024 * 1024),
    )(*args)


def passed(value, mask):
    count = lax.axis_size("dp")
    return lax.ppermute(value, "dp", [(s, s ^ mask) for s in range(count)])


def same_core():
    count = lax.axis_size("dp")
    return [list(range(c, count, 2)) for c in range(2)]


def joined(value, mask):
    return jnp.concatenate([value, passed(value, mask)], axis=0)


def halve_kernel(mine, theirs, kept, sent):
    half = kept.shape[0]
    total = mine[...] + theirs[...].astype(f32)
    kept[...] = total[:half]
    sent[...] = total[half:].astype(bf16)


def halved(kept, received):
    rows, width = kept.shape
    half = rows // 2
    return call(
        halve_kernel,
        [((half, width), f32), ((half, width), bf16)],
        [VM] * 2,
        (kept, received),
        mib=16,
    )


def over_z(value):
    count = lax.axis_size("fsdp") // HALVES
    groups = [list(range(s * count, (s + 1) * count)) for s in range(HALVES)]
    return lax.all_to_all(value, "fsdp", 0, 0, axis_index_groups=groups, tiled=True)


def other_half(value):
    count = lax.axis_size("fsdp")
    return lax.ppermute(value, "fsdp", [(s, (s + count // 2) % count) for s in range(count)])


def text_kernel(text, unit):
    t = text[...].astype(f32)
    t = t / jnp.sqrt(jnp.sum(t * t, axis=1, keepdims=True) + epsilon)
    unit[...] = t.astype(bf16)


def head_kernel(feats, weight, part):
    rows = lax.dot_general(
        feats[...], weight[...], (((0,), (0,)), ((), ())), preferred_element_type=f32
    )
    count = rows.shape[0] // 8
    along = count // HALVES
    order = [half * along + z for z in range(along) for half in range(HALVES)]
    rows = jnp.concatenate([rows[8 * k : 8 * k + 8] for k in order], axis=0)
    part[...] = rows.astype(bf16)


def sum_kernel(parts, total):
    total[...] = jnp.sum(parts[...].astype(f32), axis=0)


def unit_kernel(mine, theirs, hat, lengths, spread):
    raw = mine[...] + theirs[...]
    size = jnp.sqrt(jnp.sum(raw * raw, axis=1, keepdims=True) + epsilon)
    value = raw / size
    hat[...] = value
    lengths[...] = jnp.broadcast_to(size, lengths.shape)
    spread[...] = jnp.broadcast_to(value.astype(bf16)[None], spread.shape)


def place_of(index):
    bits = len(REDUCE)
    masks = [mask for bit, mask in enumerate(REDUCE) if index >> (bits - 1 - bit) & 1]
    return sum(1 << GATHER.index(mask) for mask in masks)


def pair_kernel(scalars, where, units, own, own_y, away, away_y, image, spread, block):
    width = units.shape[1]
    temper, offset = scalars[0], scalars[1]
    first, each = where[0], where[1]
    count = own.shape[0]
    size = 4 * count >> len(REDUCE)
    for half, pair in enumerate(((own, own_y), (away, away_y))):
        for index in range(2 * count // size):
            part, piece = divmod(place_of(2 * index) // 2, count // size)
            target = half * 2 * count + index * size
            block[target : target + size, :] = pair[part][piece * size : (piece + 1) * size, :]
    rows = units[...]
    texts = block[...]
    scores = lax.dot_general(rows, texts, (((1,), (1,)), ((), ())), preferred_element_type=f32)
    row = lax.broadcasted_iota(jnp.int32, scores.shape, 0) - first
    col = lax.broadcasted_iota(jnp.int32, scores.shape, 1)
    sign = jnp.where((row == col) & (col < each), -1.0, 1.0).astype(f32)
    logits = sign * (temper * scores + offset)
    small = jnp.exp(-jnp.abs(logits))
    losses = jnp.sum(jnp.maximum(logits, 0.0) + jnp.log1p(small), axis=1, keepdims=True)
    weights = sign * (jnp.where(logits >= 0, 1.0, small) / (1.0 + small)) * temper
    weights = weights.astype(bf16)
    spread[...] = weights
    total = jnp.dot(weights, texts, preferred_element_type=f32)
    image[:, :width] = total.astype(bf16)
    high = losses.astype(bf16).astype(f32)
    low = losses - high
    lane = lax.broadcasted_iota(jnp.int32, (rows.shape[0], 128), 1)
    image[:, width:] = jnp.where(lane == 0, high, jnp.where(lane == 1, low, 0.0)).astype(bf16)


def turn_kernel(weights, units, own, away):
    count = own.shape[0]
    for half, out in enumerate((own, away)):
        out[...] = lax.dot_general(
            weights[:, half * count : (half + 1) * count],
            units[...],
            (((0,), (0,)), ((), ())),
            preferred_element_type=f32,
        ).astype(out.dtype)


def grad_kernel(mine, theirs, hat, lengths, spread):
    width = hat.shape[1]
    total = mine[...] + theirs[...]
    direction = total[:, :width]
    value = hat[...]
    projected = jnp.sum(value * direction, axis=1, keepdims=True)
    grad = (direction - value * projected) / lengths[:, :1]
    spread[:, :, :width] = jnp.broadcast_to(
        grad.astype(bf16)[None], (spread.shape[0],) + grad.shape
    )
    tail = total[:, width:]
    lane = lax.broadcasted_iota(jnp.int32, tail.shape, 1)
    loss = jnp.sum(jnp.where(lane < 2, tail, 0.0), axis=1, keepdims=True)
    high = loss.astype(bf16).astype(f32)
    low = loss - high
    tail = jnp.where(lane == 0, high, jnp.where(lane == 1, low, 0.0)).astype(bf16)
    spread[:, :, width:] = jnp.broadcast_to(tail[None], (spread.shape[0],) + tail.shape)


def body(pooled_feats, head_weight, text_embed, logit_scale, logit_bias):
    each, width = text_embed.shape
    rows, deep = pooled_feats.shape
    members = lax.axis_size("fsdp")
    chips = lax.axis_size("dp") // 2
    core = lax.axis_index("dp") % 2
    member_id = lax.axis_index("fsdp")
    along, both = members // HALVES, HALVES * each
    first = (member_id % along * HALVES + member_id // along) * each
    wide = width + 128

    (text_unit,) = call(text_kernel, [((each, width), bf16)], [VM], (text_embed,))
    with jax.named_scope("text_gather"):
        far, near = GATHER[:2]
        own = [text_unit] + [passed(text_unit, mask) for mask in (far, near, far + near)]
        own = joined(joined(jnp.concatenate(own, axis=0), GATHER[2]), GATHER[3])
        last = GATHER[4]
        blocks = [own] + [passed(own, mask) for mask in (last, CORE, last + CORE)]
    (part,) = call(head_kernel, [((rows, width), bf16)], [VM] * 2, (pooled_feats.T, head_weight))
    with jax.named_scope("head_reduce"):
        parts = over_z(part).reshape(along, both, width)
        (mine,) = call(sum_kernel, [((both, width), f32)], [VM], (parts,))
        theirs = other_half(mine)
    hat, lengths, unit_spread = call(
        unit_kernel,
        [((both, width), f32), ((both, 128), f32), ((along, both, width), bf16)],
        [VM] * 2,
        (mine, theirs),
    )
    with jax.named_scope("unit_gather"):
        units = over_z(unit_spread.reshape(rows, width))
    image, weights = pl.pallas_call(
        pair_kernel,
        out_shape=[
            jax.ShapeDtypeStruct((rows, wide), bf16),
            jax.ShapeDtypeStruct((rows, 2 * chips * each), bf16),
        ],
        in_specs=[SM, SM] + [VM] * 5,
        out_specs=[VM, VM],
        scratch_shapes=[pltpu.VMEM((2 * chips * each, width), bf16)],
        compiler_params=pltpu.CompilerParams(vmem_limit_bytes=16 * 1024 * 1024),
    )(
        jnp.concatenate([logit_scale, logit_bias]),
        jnp.stack([first, jnp.int32(each)]).astype(jnp.int32),
        units,
        *blocks,
    )
    text_own, text_away = call(
        turn_kernel,
        [((chips * each, width), f32), ((chips * each, width), bf16)],
        [VM, VM],
        (weights, units),
        mib=16,
    )
    with jax.named_scope("text_reduce"):
        kept, sent = halved(text_own, passed(text_away, CORE))
    with jax.named_scope("image_reduce"):
        parts = over_z(image).reshape(along, both, wide)
        kept, sent, parts = lax.optimization_barrier((kept, sent, parts))
        (mine,) = call(sum_kernel, [((both, wide), f32)], [VM], (parts,))
        theirs = other_half(mine)
    with jax.named_scope("text_reduce"):
        received = passed(sent, REDUCE[0])
    (grad_spread,) = call(
        grad_kernel,
        [((along, both, wide), bf16)],
        [VM] * 4,
        (mine, theirs, hat, lengths),
    )
    with jax.named_scope("text_reduce"):
        kept, received, grad_spread = lax.optimization_barrier((kept, received, grad_spread))
        kept, sent = halved(kept, received)
        kept, sent = halved(kept, passed(sent, REDUCE[1]))
    with jax.named_scope("grad_gather"):
        grads = over_z(grad_spread.reshape(rows, wide))
    losses = grads[:, width].astype(f32) + grads[:, width + 1].astype(f32)
    unit_grad = grads[:, :width]
    kept, sent, unit_grad = lax.optimization_barrier((kept, sent, unit_grad))
    with jax.named_scope("text_reduce"):
        received = passed(sent, REDUCE[2])
    by_z = pooled_feats.reshape(HALVES, along, each, deep).swapaxes(0, 1).reshape(rows, deep)
    head_part = lax.dot_general(
        unit_grad, by_z, (((0,), (0,)), ((), ())), preferred_element_type=f32
    )
    cols = width // (2 * chips)
    head_part = head_part.reshape(chips, 2, cols, deep)
    mine = lax.dynamic_index_in_dim(head_part, core, 1, keepdims=False)
    away = lax.dynamic_index_in_dim(head_part, 1 - core, 1, keepdims=False)
    with jax.named_scope("head_swap"):
        mine = mine + passed(away.astype(bf16), 1).astype(f32)
    mine = mine.astype(bf16)
    with jax.named_scope("text_reduce"):
        kept, received, unit_grad, mine = lax.optimization_barrier(
            (kept, received, unit_grad, mine)
        )
        kept, sent = halved(kept, received)
        kept, sent = halved(kept, passed(sent, REDUCE[3]))
        received = passed(sent, REDUCE[4])
    with jax.named_scope("last_reduce"):
        mine = lax.all_to_all(mine, "dp", 0, 0, axis_index_groups=same_core(), tiled=True)
    pooled_grad = lax.dot_general(
        unit_grad, head_weight, (((1,), (1,)), ((), ())), preferred_element_type=f32
    )
    kept, received, mine = lax.optimization_barrier((kept, received, mine))
    text_grad = kept + received.astype(f32)
    head_grad = jnp.sum(mine.astype(f32), axis=0).T
    losses = losses.reshape(along, HALVES, each).swapaxes(0, 1).reshape(rows)
    pooled_grad = pooled_grad.reshape(along, HALVES, each, deep).swapaxes(0, 1).reshape(rows, deep)
    return (losses, head_grad, pooled_grad, text_grad)


def solution(mesh):
    return jax.shard_map(
        body,
        mesh=mesh,
        in_specs=(P("dp", "fsdp"), P("fsdp", None), P(("dp", "fsdp"), None), P(), P()),
        out_specs=(P("dp"), P("fsdp", "dp"), P("dp", "fsdp"), P(("dp", "fsdp"), None)),
        check_vma=False,
    )
```

```python
import jax
import jax.numpy as jnp
from jax import lax
from jax.experimental import pallas as pl
from jax.experimental.pallas import tpu as pltpu
from jax.sharding import PartitionSpec as P

epsilon = 1e-06
bf16 = jnp.bfloat16
f32 = jnp.float32
VM = pl.BlockSpec(memory_space=pltpu.VMEM)
SM = pl.BlockSpec(memory_space=pltpu.SMEM)
GATHER = (32, 16, 8, 4, 2)
REDUCE = (2, 4, 16, 8, 32)
CORE = 1
HALVES = 2


def call(kernel, outs, in_specs, args, mib=8):
    return pl.pallas_call(
        kernel,
        out_shape=[jax.ShapeDtypeStruct(s, d) for s, d in outs],
        in_specs=in_specs,
        out_specs=[VM] * len(outs),
        compiler_params=pltpu.CompilerParams(vmem_limit_bytes=mib * 1024 * 1024),
    )(*args)


def passed(value, mask):
    count = lax.axis_size("dp")
    return lax.ppermute(value, "dp", [(s, s ^ mask) for s in range(count)])


def same_core():
    count = lax.axis_size("dp")
    return [list(range(c, count, 2)) for c in range(2)]


def joined(value, mask):
    return jnp.concatenate([value, passed(value, mask)], axis=0)


def halves_passed(value, mask):
    size = value.shape[0] // 2
    return value[:size], passed(value[size:].astype(bf16), mask)


def halves_added(pair):
    return pair[0] + pair[1].astype(f32)


def over_z(value):
    count = lax.axis_size("fsdp") // HALVES
    groups = [list(range(s * count, (s + 1) * count)) for s in range(HALVES)]
    return lax.all_to_all(value, "fsdp", 0, 0, axis_index_groups=groups, tiled=True)


def other_half(value):
    count = lax.axis_size("fsdp")
    return lax.ppermute(value, "fsdp", [(s, (s + count // 2) % count) for s in range(count)])


def text_kernel(text, unit):
    t = text[...].astype(f32)
    t = t / jnp.sqrt(jnp.sum(t * t, axis=1, keepdims=True) + epsilon)
    unit[...] = t.astype(bf16)


def head_kernel(feats, weight, part):
    rows = lax.dot_general(
        feats[...], weight[...], (((0,), (0,)), ((), ())), preferred_element_type=f32
    )
    count = rows.shape[0] // 8
    along = count // HALVES
    order = [half * along + z for z in range(along) for half in range(HALVES)]
    rows = jnp.concatenate([rows[8 * k : 8 * k + 8] for k in order], axis=0)
    part[...] = rows.astype(bf16)


def sum_kernel(parts, total):
    total[...] = jnp.sum(parts[...].astype(f32), axis=0)


def unit_kernel(mine, theirs, hat, lengths, spread):
    raw = mine[...] + theirs[...]
    size = jnp.sqrt(jnp.sum(raw * raw, axis=1, keepdims=True) + epsilon)
    value = raw / size
    hat[...] = value
    lengths[...] = jnp.broadcast_to(size, lengths.shape)
    spread[...] = jnp.broadcast_to(value.astype(bf16)[None], spread.shape)


def place_of(index):
    bits = len(REDUCE)
    masks = [mask for bit, mask in enumerate(REDUCE) if index >> (bits - 1 - bit) & 1]
    return sum(1 << GATHER.index(mask) for mask in masks)


def pair_kernel(scalars, where, units, own, own_y, away, away_y, image, spread, block):
    width = units.shape[1]
    temper, offset = scalars[0], scalars[1]
    first, each = where[0], where[1]
    count = own.shape[0]
    size = 4 * count >> len(REDUCE)
    for half, pair in enumerate(((own, own_y), (away, away_y))):
        for index in range(2 * count // size):
            part, piece = divmod(place_of(2 * index) // 2, count // size)
            target = half * 2 * count + index * size
            block[target : target + size, :] = pair[part][piece * size : (piece + 1) * size, :]
    rows = units[...]
    texts = block[...]
    scores = lax.dot_general(rows, texts, (((1,), (1,)), ((), ())), preferred_element_type=f32)
    row = lax.broadcasted_iota(jnp.int32, scores.shape, 0) - first
    col = lax.broadcasted_iota(jnp.int32, scores.shape, 1)
    sign = jnp.where((row == col) & (col < each), -1.0, 1.0).astype(f32)
    logits = sign * (temper * scores + offset)
    small = jnp.exp(-jnp.abs(logits))
    losses = jnp.sum(jnp.maximum(logits, 0.0) + jnp.log1p(small), axis=1, keepdims=True)
    weights = sign * (jnp.where(logits >= 0, 1.0, small) / (1.0 + small)) * temper
    weights = weights.astype(bf16)
    spread[...] = weights
    total = jnp.dot(weights, texts, preferred_element_type=f32)
    image[:, :width] = total.astype(bf16)
    high = losses.astype(bf16).astype(f32)
    low = losses - high
    lane = lax.broadcasted_iota(jnp.int32, (rows.shape[0], 128), 1)
    image[:, width:] = jnp.where(lane == 0, high, jnp.where(lane == 1, low, 0.0)).astype(bf16)


def turn_kernel(weights, units, own, away):
    count = own.shape[0]
    for half, out in enumerate((own, away)):
        out[...] = lax.dot_general(
            weights[:, half * count : (half + 1) * count],
            units[...],
            (((0,), (0,)), ((), ())),
            preferred_element_type=f32,
        ).astype(out.dtype)


def grad_kernel(mine, theirs, hat, lengths, spread):
    width = hat.shape[1]
    total = mine[...] + theirs[...]
    direction = total[:, :width]
    value = hat[...]
    projected = jnp.sum(value * direction, axis=1, keepdims=True)
    grad = (direction - value * projected) / lengths[:, :1]
    spread[:, :, :width] = jnp.broadcast_to(
        grad.astype(bf16)[None], (spread.shape[0],) + grad.shape
    )
    tail = total[:, width:]
    lane = lax.broadcasted_iota(jnp.int32, tail.shape, 1)
    loss = jnp.sum(jnp.where(lane < 2, tail, 0.0), axis=1, keepdims=True)
    high = loss.astype(bf16).astype(f32)
    low = loss - high
    tail = jnp.where(lane == 0, high, jnp.where(lane == 1, low, 0.0)).astype(bf16)
    spread[:, :, width:] = jnp.broadcast_to(tail[None], (spread.shape[0],) + tail.shape)


def body(pooled_feats, head_weight, text_embed, logit_scale, logit_bias):
    each, width = text_embed.shape
    rows, deep = pooled_feats.shape
    members = lax.axis_size("fsdp")
    chips = lax.axis_size("dp") // 2
    core = lax.axis_index("dp") % 2
    member_id = lax.axis_index("fsdp")
    along, both = members // HALVES, HALVES * each
    first = (member_id % along * HALVES + member_id // along) * each
    wide = width + 128

    (text_unit,) = call(text_kernel, [((each, width), bf16)], [VM], (text_embed,))
    with jax.named_scope("text_gather"):
        own = joined(text_unit, GATHER[0])
        own, pooled_feats = lax.optimization_barrier((own, pooled_feats))
        for mask in GATHER[1:4]:
            own = joined(own, mask)
        last = GATHER[4]
        blocks = [own] + [passed(own, mask) for mask in (last, CORE, last + CORE)]
    (part,) = call(head_kernel, [((rows, width), bf16)], [VM] * 2, (pooled_feats.T, head_weight))
    with jax.named_scope("head_reduce"):
        parts = over_z(part).reshape(along, both, width)
        (mine,) = call(sum_kernel, [((both, width), f32)], [VM], (parts,))
        theirs = other_half(mine)
    hat, lengths, unit_spread = call(
        unit_kernel,
        [((both, width), f32), ((both, 128), f32), ((along, both, width), bf16)],
        [VM] * 2,
        (mine, theirs),
    )
    with jax.named_scope("unit_gather"):
        units = over_z(unit_spread.reshape(rows, width))
    image, weights = pl.pallas_call(
        pair_kernel,
        out_shape=[
            jax.ShapeDtypeStruct((rows, wide), bf16),
            jax.ShapeDtypeStruct((rows, 2 * chips * each), bf16),
        ],
        in_specs=[SM, SM] + [VM] * 5,
        out_specs=[VM, VM],
        scratch_shapes=[pltpu.VMEM((2 * chips * each, width), bf16)],
        compiler_params=pltpu.CompilerParams(vmem_limit_bytes=16 * 1024 * 1024),
    )(
        jnp.concatenate([logit_scale, logit_bias]),
        jnp.stack([first, jnp.int32(each)]).astype(jnp.int32),
        units,
        *blocks,
    )
    text_own, text_away = call(
        turn_kernel,
        [((chips * each, width), f32), ((chips * each, width), bf16)],
        [VM, VM],
        (weights, units),
        mib=16,
    )
    with jax.named_scope("text_reduce"):
        text_sum = halves_added((text_own, passed(text_away, CORE)))
        size = text_sum.shape[0] // 4
        block = [text_sum[k * size : (k + 1) * size] for k in range(4)]
        sent = [block[0]] + [
            passed(piece.astype(bf16), mask)
            for piece, mask in zip(block[1:], (REDUCE[1], REDUCE[0], REDUCE[0] + REDUCE[1]))
        ]
    with jax.named_scope("image_reduce"):
        parts = over_z(image).reshape(along, both, wide)
        (mine,) = call(sum_kernel, [((both, wide), f32)], [VM], (parts,))
        theirs = other_half(mine)
    (grad_spread,) = call(
        grad_kernel,
        [((along, both, wide), bf16)],
        [VM] * 4,
        (mine, theirs, hat, lengths),
    )
    sent, _ = lax.optimization_barrier((sent, grad_spread))
    with jax.named_scope("text_reduce"):
        text_sum = sent[0] + sum(piece.astype(f32) for piece in sent[1:])
        text_sum = halves_added(halves_passed(text_sum, REDUCE[2]))
        sent = halves_passed(text_sum, REDUCE[3])
    with jax.named_scope("grad_gather"):
        grads = over_z(grad_spread.reshape(rows, wide))
    unit_grad = grads[:, :width]
    losses = grads[:, width].astype(f32) + grads[:, width + 1].astype(f32)
    by_z = pooled_feats.reshape(HALVES, along, each, deep).swapaxes(0, 1).reshape(rows, deep)
    head_part = lax.dot_general(
        unit_grad, by_z, (((0,), (0,)), ((), ())), preferred_element_type=f32
    )
    cols = width // (2 * chips)
    head_part = head_part.reshape(chips, 2, cols, deep)
    mine = lax.dynamic_index_in_dim(head_part, core, 1, keepdims=False)
    away = lax.dynamic_index_in_dim(head_part, 1 - core, 1, keepdims=False)
    with jax.named_scope("head_swap"):
        mine = mine + passed(away.astype(bf16), 1).astype(f32)
    mine = mine.astype(bf16)
    sent, _ = lax.optimization_barrier((sent, mine))
    with jax.named_scope("text_reduce"):
        sent = halves_passed(halves_added(sent), REDUCE[4])
    unit_grad, mine = lax.optimization_barrier((unit_grad, mine))
    with jax.named_scope("last_reduce"):
        mine = lax.all_to_all(mine, "dp", 0, 0, axis_index_groups=same_core(), tiled=True)
    pooled_grad = lax.dot_general(
        unit_grad, head_weight, (((1,), (1,)), ((), ())), preferred_element_type=f32
    )
    sent, mine = lax.optimization_barrier((sent, mine))
    text_grad = halves_added(sent)
    head_grad = jnp.sum(mine.astype(f32), axis=0).T
    losses = losses.reshape(along, HALVES, each).swapaxes(0, 1).reshape(rows)
    pooled_grad = pooled_grad.reshape(along, HALVES, each, deep).swapaxes(0, 1).reshape(rows, deep)
    return (losses, head_grad, pooled_grad, text_grad)


def solution(mesh):
    return jax.shard_map(
        body,
        mesh=mesh,
        in_specs=(P("dp", "fsdp"), P("fsdp", None), P(("dp", "fsdp"), None), P(), P()),
        out_specs=(P("dp"), P("fsdp", "dp"), P("dp", "fsdp"), P(("dp", "fsdp"), None)),
        check_vma=False,
    )
```
